32 devices in a mesh: gx: 2 (over x), gy: 8 (over z, y), lev: 2 (over core).
Axes of the slice: x: 2, y: 2, z: 4, core: 2. Of those that a mesh axis runs over, the one named last changes fastest.
Arguments:
- source: float32 [32, 256, 256], P('lev', 'gy', 'gx'), may hold values from -6 to 6
- remap_weights: float32 [512, 4, 128, 128], P(('gx', 'gy'))
- intersection_devices: int32 [512, 4], replicated, may hold values from 0 to 15, all different within a row; in each aligned block of 32 rows (0 to 31, 32 to 63, ...) at most 16 rows name the same one
- intersection_rows: int32 [512, 4], replicated, may hold values from 0 to 31
- smoothing: float32 [64, 1024], P('gx', 'gy'), may hold values from 0.04 to 0.24
Outputs:
- face_field: float32 [32, 64, 1024], P('lev', 'gx', 'gy')
The draws below stay inside these ranges and needn't reach their ends.
Inputs may be any that keep to these rules, and one draw needn't show every extreme that they name: `intersection_devices`: each row names 4 different source tiles. Among the rows of one destination device (32 aligned rows), no source tile is named more than 16 times, and in every draw some source tile is named exactly 16 times.
All inputs are finite; a program needn't handle non-finite values.
Results may differ from the reference program's by a relative error of at most 0.00011.
Values sent between devices are 32-bit elements; how exact they have to be, the bound alone decides.
A program may use at most 64 MiB of HBM per device.

```python
import math
import jax
import jax.numpy as jnp
import numpy as np
from jax import lax

BLOCK = 128
K = 4
PASSES = 3
SLAT = 32
FX = 32
CAP = 16
LEV = 32
NLAT = 256
NLON = 256
NX = 64
NY = 1024
NROWS = 512
N_GX = 2
N_GY = 8


def draw_remap_weights(key, part):
    key_diag = jax.random.fold_in(key, 11)
    key_off = jax.random.fold_in(key, 12)
    gains = jax.random.uniform(key_diag, (NROWS, K, 1, BLOCK), jnp.float32, 0.6, 1.4)
    spread = jax.random.uniform(key_off, (NROWS, K, BLOCK, BLOCK), jnp.float32, 0.0, 2.0)
    diagonal = (jnp.arange(BLOCK)[:, None] == jnp.arange(BLOCK)[None, :]).astype(jnp.float32)
    return 0.5 / K * gains * diagonal + 0.5 / (K * BLOCK) * spread


def place_ends(entries, stream_key, least, largest):
    extent = entries.shape
    index_at = [jax.random.randint(jax.random.fold_in(stream_key, axis), (), 0, extent[axis]) for axis in range(len(extent))]
    entries = entries.at[tuple(index_at)].set(least)
    longest = extent.index(max(extent))
    index_at[longest] = (index_at[longest] + 1) % extent[longest]
    return entries.at[tuple(index_at)].set(largest)


def levels(rng, extent, pieces, least, high):
    def one(dim, shards_of):
        heights = jax.random.uniform(jax.random.fold_in(jax.random.fold_in(rng, 6), dim), (shards_of,), jnp.float32, least / len(pieces), high / len(pieces))
        return jnp.repeat(jnp.exp(heights), extent[dim] // shards_of).reshape((-1,) + (1,) * (len(extent) - dim - 1))

    factor_of = one(*pieces[0])
    for cut in pieces[1:]:
        factor_of = factor_of * one(*cut)
    return factor_of


def routed_block(rng, own, number, rows, count, top, most, slope):
    sequence = jax.random.permutation(rng, count)
    packed, ordinary = load_shares(count, rows * top, most, slope, True), load_shares(count, rows * top, most, slope, False)
    places = jnp.arange(count)

    def named(tallies, turn):
        used = int((tallies > 0).sum())
        fixed = max(1, used // 4)
        moved = fixed + (places - fixed + turn * (used - fixed)) % max(1, count - fixed)
        return jnp.zeros((count,), jnp.int32).at[sequence[jnp.where(places < fixed, places, moved)]].set(jnp.asarray(tallies, jnp.int32))

    tallies = jnp.where(number % 4 == 0, named(packed, number // 4), named(ordinary, number - number // 4 - 1))
    mixed = jax.random.permutation(jax.random.fold_in(own, 3), count)
    source_of, sink = mixed[0:count // 2 * 2:2], mixed[1:count // 2 * 2:2]
    slack = jnp.minimum(tallies[source_of] - 1, most - tallies[sink]) // 2
    slack = jnp.where((source_of == sequence[0]) | (sink == sequence[0]) | (tallies[sink] == 0), 0, jnp.maximum(slack, 0))
    moved = jax.random.randint(jax.random.fold_in(own, 4), (count // 2,), 0, 1 << 20) % (slack + 1)
    tallies = tallies.at[source_of].add(-moved).at[sink].add(moved)
    members = jnp.searchsorted(jnp.cumsum(tallies), jnp.arange(rows * top), side="right").astype(jnp.int32)
    grid = members.reshape(top, rows).T
    grid = grid[jax.random.permutation(jax.random.fold_in(own, 1), rows)]
    turn = jax.random.randint(jax.random.fold_in(own, 2), (rows, 1), 0, top)
    return jnp.take_along_axis(grid, (jnp.arange(top)[None, :] + turn) % top, axis=1)


def load_shares(count, total, reach, lean, full):
    portions = [(1 << 20) // math.isqrt(rank ** lean) + 1 for rank in range(1, count + 1)]
    largest = reach if full else min(reach, max(-(-total // count), total * portions[0] // sum(portions)))
    least = 1 if total - largest >= count - 1 else 0
    given, spare = [largest] + [least] * (count - 1), total - largest - least * (count - 1)
    while spare > 0:
        movable = [i for i in range(1, count) if given[i] < largest] or [i for i in range(1, count) if given[i] < reach]
        pool, remaining = sum([portions[i] for i in movable]), spare
        for i in movable:
            addition = min(reach - given[i], max(1, remaining * portions[i] // pool), spare)
            given[i] = given[i] + addition
            spare = spare - addition
    return np.array(given)


def noise(stream_key, dims, scale, most, pieces=(), dtype=jnp.bfloat16):
    level = levels(stream_key, dims, pieces, -0.22, 0.18) if pieces else 1.0
    drawn = jax.random.normal(stream_key, dims, jnp.float32) * scale * level
    return jnp.minimum(jnp.maximum(drawn, -most), most).astype(dtype)


def setup_inputs(seed: int = 0) -> dict:
    keys = jax.random.split(jax.random.key(seed), 6)
    source = noise(keys[0], (LEV, NLAT, NLON), 1.0, 6.0, ((0, 2), (1, 8), (2, 2)), jnp.float32)
    remap_weights = draw_remap_weights(jax.random.fold_in(keys[5], 71), 0)
    intersection_devices_keys = jax.random.split(jax.random.fold_in(keys[2], 1), NROWS // FX)
    intersection_devices_turns = jax.random.permutation(jax.random.fold_in(keys[2], 3), NROWS // FX)
    intersection_devices = jax.vmap(lambda own, number: routed_block(jax.random.fold_in(keys[2], 2), own, number, FX, N_GX * N_GY, K, CAP, 1))(intersection_devices_keys, intersection_devices_turns).reshape((NROWS, K))
    intersection_rows = place_ends(jax.random.randint(keys[3], (NROWS, K), 0, SLAT), jax.random.fold_in(keys[3], 1), 0, SLAT - 1).astype(jnp.int32)
    smoothing = jnp.clip(0.04 + 0.19999999552965164 * jax.random.uniform(keys[4], (NX, NY), jnp.float32) ** levels(keys[4], (NX, NY), ((0, 2), (1, 8)), -0.2, 0.2), 0.04, 0.24)
    return {"source": source, "remap_weights": remap_weights, "intersection_devices": intersection_devices, "intersection_rows": intersection_rows, "smoothing": smoothing}


def reference(source, remap_weights, intersection_devices, intersection_rows, smoothing):
    devices = N_GX * N_GY
    grouped = source.reshape(LEV, N_GY, SLAT, N_GX, BLOCK)
    lon_tile = (intersection_devices // N_GY).reshape(devices, FX, K)
    lat_tile = (intersection_devices % N_GY).reshape(devices, FX, K)
    lat_rows = intersection_rows.reshape(devices, FX, K)
    weights = remap_weights.reshape(devices, FX, K, BLOCK, BLOCK)

    def per_device(item):
        lon_part, lat_part, row_part, weight_part = item
        blocks = grouped[:, lat_part, row_part, lon_part, :]
        return jnp.einsum("likc,ikcd->lid", blocks, weight_part, precision=lax.Precision.HIGHEST)

    result = lax.map(per_device, (lon_tile, lat_tile, lat_rows, weights))
    field = result.reshape(N_GX, N_GY, LEV, FX, BLOCK).transpose(2, 0, 3, 1, 4).reshape(LEV, NX, NY)
    for _ in range(PASSES):
        padded = jnp.pad(field, ((0, 0), (1, 1), (1, 1)))
        laplace = padded[:, 2:, 1:-1] + padded[:, :-2, 1:-1] + padded[:, 1:-1, 2:] + padded[:, 1:-1, :-2] - 4.0 * field
        field = field + smoothing * laplace
    return field
```

```python
import functools

import jax
import jax.numpy as jnp
from jax import lax
from jax.experimental import pallas as pl
from jax.experimental.pallas import tpu as pltpu
from jax.sharding import PartitionSpec as P

PASSES = 3
MESH = pl.DeviceIdType.MESH
DIRS = [(dx, dy) for dx in (-1, 0, 1) for dy in (-1, 0, 1) if (dx, dy) != (0, 0)]
OPPOSITE = [DIRS.index((-dx, -dy)) for dx, dy in DIRS]
LANES = 128
STRIP = 8
PER_TILE = LANES // STRIP


def layout(along_x, along_y, capacity, rows):
    inner = 2 if along_y % 2 == 0 else 1
    if capacity * inner * along_x > rows:
        return along_y // inner, inner
    return 1, along_y


def kernel(dims, send_rows, pick, src, weights, smooth, out, inbox, outbox, w_full, w_high, w_low,
           main_a, main_b, side_a, side_b, s_main, s_side, s_in, edge, edge_in,
           send_sem, recv_sem, chain_send, chain_recv, s_send, s_recv, h_send, h_recv, w_sem, *chain):
    along_x, along_y, depth, inner, capacity = dims
    frows, fan = w_full.shape[0], pick.shape[0] // w_full.shape[0]
    levels = src.shape[1]
    columns = along_x * inner
    ups, downs = chain[: depth - 1], chain[depth - 1:]
    x, y, lev = lax.axis_index("gx"), lax.axis_index("gy"), lax.axis_index("lev")
    z, yi = y // inner, y % inner
    column = x * inner + yi
    lane = lax.broadcasted_iota(jnp.int32, (levels, LANES), 1)

    def column_id(c):
        return (c // inner, z * inner + c % inner, lev)

    def near(dx, dy):
        ok = jnp.logical_and(
            jnp.logical_and(x + dx >= 0, x + dx < along_x),
            jnp.logical_and(y + dy >= 0, y + dy < along_y),
        )
        return ok, (x + dx, y + dy, lev)

    barrier = pltpu.get_barrier_semaphore()

    def greet(device):
        pl.semaphore_signal(barrier, inc=1, device_id=device, device_id_type=MESH)

    def greet_column(q, carry):
        greet(column_id(lax.rem(column + q, columns)))
        return carry

    lax.fori_loop(1, columns, greet_column, 0)
    total = columns - 1
    links = [near(dx, dy) for dx, dy in DIRS]
    if depth > 1:
        links = links + [(z < depth - 1, (x, y + inner, lev)), (z > 0, (x, y - inner, lev))]
    for ok, device in links:
        total = total + ok.astype(jnp.int32)

        @pl.when(ok)
        def _():
            greet(device)

    w_copy = pltpu.make_async_copy(weights, w_full, w_sem)
    w_copy.start()
    pl.semaphore_wait(barrier, total)

    def chain_copy(up, t):
        source = src if t == 0 else (ups if up else downs)[t - 1]
        step = inner if up else -inner
        return pltpu.make_async_remote_copy(
            src_ref=source, dst_ref=(ups if up else downs)[t],
            send_sem=chain_send.at[0 if up else 1, t], recv_sem=chain_recv.at[0 if up else 1, t],
            device_id=(x, y + step, lev), device_id_type=MESH)

    def slot_copy(q, tile):
        c = lax.rem(column + q, columns)
        return pltpu.make_async_remote_copy(
            src_ref=outbox.at[pl.ds((c * depth + tile) * capacity, capacity)],
            dst_ref=inbox.at[pl.ds((column * depth + tile) * capacity, capacity)],
            send_sem=send_sem.at[q * depth + tile], recv_sem=recv_sem.at[q * depth + tile],
            device_id=column_id(c), device_id_type=MESH)

    def ship(chunk, tile):
        def peer(q, carry):
            base = (lax.rem(column + q, columns) * depth + tile) * capacity
            for j in range(capacity):
                outbox[base + j] = chunk[send_rows[base + j]]
            slot_copy(q, tile).start()
            return carry

        lax.fori_loop(1, columns, peer, 0)
        base = (column * depth + tile) * capacity
        for j in range(capacity):
            inbox[base + j] = chunk[send_rows[base + j]]

    if depth > 1:
        @pl.when(z < depth - 1)
        def _():
            chain_copy(True, 0).start()

        @pl.when(z > 0)
        def _():
            chain_copy(False, 0).start()

    ship(src, z)

    def s_copy(k):
        ok, device = near(*DIRS[k])
        return ok, pltpu.make_async_remote_copy(
            src_ref=smooth, dst_ref=s_in.at[OPPOSITE[k]], send_sem=s_send.at[k],
            recv_sem=s_recv.at[OPPOSITE[k]], device_id=device, device_id_type=MESH)

    def h_copy(k):
        dx, dy = DIRS[k]
        ok, device = near(dx, dy)
        if dy == 0:
            source = main_a.at[pl.ds(frows if dx > 0 else PASSES, PASSES)]
            target = main_a.at[pl.ds(0 if dx > 0 else frows + PASSES, PASSES)]
        else:
            source, target = edge, edge_in.at[OPPOSITE[k]]
        return ok, pltpu.make_async_remote_copy(
            src_ref=source, dst_ref=target, send_sem=h_send.at[k],
            recv_sem=h_recv.at[OPPOSITE[k]], device_id=device, device_id_type=MESH)

    def arrival(make, k):
        return make(OPPOSITE[k])[1]

    for k in range(len(DIRS)):
        ok, copy = s_copy(k)

        @pl.when(ok)
        def _():
            copy.start()

    for k, (dx, dy) in enumerate(DIRS):
        ok, _ = near(dx, dy)

        @pl.when(jnp.logical_not(ok))
        def _():
            s_in[k] = jnp.zeros(s_in.shape[1:], jnp.float32)
            if dy == 0:
                main_a[pl.ds(0 if dx < 0 else frows + PASSES, PASSES)] = jnp.zeros(
                    (PASSES,) + main_a.shape[1:], jnp.float32)
            else:
                edge_in[k] = jnp.zeros(edge_in.shape[1:], jnp.float32)

    for t in range(depth - 1):
        for up, ok, onward in ((True, z >= t + 1, z < depth - 1), (False, z + 1 + t <= depth - 1, z > 0)):
            @pl.when(ok)
            def _():
                chain_copy(up, t).wait_recv()
                if t + 1 < depth - 1:
                    @pl.when(onward)
                    def _():
                        chain_copy(up, t + 1).start()
                ship((ups if up else downs)[t], z - 1 - t if up else z + 1 + t)
        if t == 0:
            split_weights(w_copy, w_full, w_high, w_low)
    if depth == 1:
        split_weights(w_copy, w_full, w_high, w_low)

    for k in range(len(DIRS)):
        ok, copy = s_copy(k)

        @pl.when(ok)
        def _():
            copy.wait_send()
            arrival_wait(s_in.at[k], smooth, s_recv.at[k])

    row_lane = lax.broadcasted_iota(jnp.int32, (1, LANES), 1)

    def side(left, right):
        return jnp.where(row_lane < PASSES, right, jnp.where(row_lane >= LANES - PASSES, left, 0.0))

    at = {d: k for k, d in enumerate(DIRS)}
    for i in range(frows):
        s_main[PASSES + i] = smooth[i:i + 1, :]
        s_side[PASSES + i] = side(s_in[at[0, -1], i:i + 1, :], s_in[at[0, 1], i:i + 1, :])
    for i in range(PASSES):
        low, high = frows - PASSES + i, frows + PASSES + i
        s_main[i] = s_in[at[-1, 0], low:low + 1, :]
        s_side[i] = side(s_in[at[-1, -1], low:low + 1, :], s_in[at[-1, 1], low:low + 1, :])
        s_main[high] = s_in[at[1, 0], i:i + 1, :]
        s_side[high] = side(s_in[at[1, -1], i:i + 1, :], s_in[at[1, 1], i:i + 1, :])

    def landed(n, carry):
        slot_copy(n // depth, lax.rem(n, depth)).wait_recv()
        return carry

    lax.fori_loop(depth, columns * depth, landed, 0)

    def product(i):
        blocks = jnp.concatenate([inbox[pick[i * fan + k]] for k in range(fan)], axis=1)
        high = blocks.astype(jnp.bfloat16)
        low = (blocks - high.astype(jnp.float32)).astype(jnp.bfloat16)
        both = jnp.dot(jnp.concatenate([high, low], axis=0), w_high[i], preferred_element_type=jnp.float32)
        rest = jnp.dot(high, w_low[i], preferred_element_type=jnp.float32)
        main_a[PASSES + i] = both[:levels] + (both[levels:] + rest)

    def products(n, carry):
        for j in range(4):
            product(n * 4 + j)
        return carry

    lax.fori_loop(0, frows // 4, products, 0)

    for k, (dx, dy) in enumerate(DIRS):
        if dy == 0:
            ok, copy = h_copy(k)

            @pl.when(ok)
            def _():
                copy.start()

    tiles = frows // PER_TILE
    for b in range(tiles):
        packed = jnp.zeros((levels, LANES), jnp.float32)
        for j in range(PER_TILE):
            moved = pltpu.roll(main_a[PASSES + b * PER_TILE + j], STRIP * j + STRIP // 2, axis=1)
            packed = jnp.where(lane // STRIP == j, moved, packed)
        edge[b] = packed
    for k, (dx, dy) in enumerate(DIRS):
        if dy != 0:
            ok, copy = h_copy(k)

            @pl.when(ok)
            def _():
                copy.start()

    def sent(n, carry):
        slot_copy(n // depth, lax.rem(n, depth)).wait_send()
        return carry

    lax.fori_loop(depth, columns * depth, sent, 0)
    for t in range(depth - 1):
        @pl.when(jnp.logical_and(z < depth - 1, z - t >= 0))
        def _():
            chain_copy(True, t).wait_send()

        @pl.when(jnp.logical_and(z > 0, z + t <= depth - 1))
        def _():
            chain_copy(False, t).wait_send()

    for k, (dx, dy) in enumerate(DIRS):
        ok, copy = h_copy(k)

        @pl.when(ok)
        def _():
            copy.wait_send()
            if dy == 0:
                rows = main_a.at[pl.ds(0 if dx < 0 else frows + PASSES, PASSES)]
                arrival_wait(rows, rows, h_recv.at[k])
            else:
                arrival_wait(edge_in.at[k], edge, h_recv.at[k])

    inside = jnp.logical_or(lane < PASSES, lane >= LANES - PASSES)

    def unpack(row, tile, place, left, right):
        merged = jnp.where(lax.rem(lane, STRIP) < STRIP // 2, edge_in[left, tile], edge_in[right, tile])
        moved = pltpu.roll(merged, (2 * LANES - STRIP * place - STRIP // 2) % LANES, axis=1)
        side_a[row] = jnp.where(inside, moved, 0.0)

    for i in range(frows):
        unpack(PASSES + i, i // PER_TILE, i % PER_TILE, at[0, -1], at[0, 1])
    for i in range(PASSES):
        far = frows - PASSES + i
        unpack(i, far // PER_TILE, far % PER_TILE, at[-1, -1], at[-1, 1])
        unpack(frows + PASSES + i, 0, i, at[1, -1], at[1, 1])

    first, last = lane == 0, lane == LANES - 1

    def smooth_row(r, main, sides, write):
        u, h = main[r], sides[r]
        u_up, u_down = pltpu.roll(u, 1, axis=1), pltpu.roll(u, LANES - 1, axis=1)
        h_up, h_down = pltpu.roll(h, 1, axis=1), pltpu.roll(h, LANES - 1, axis=1)
        lap = (main[r + 1] + main[r - 1] + jnp.where(last, h_down, u_down)
               + jnp.where(first, h_up, u_up) - 4.0 * u)
        lap_h = (sides[r + 1] + sides[r - 1] + jnp.where(last, u_down, h_down)
                 + jnp.where(first, u_up, h_up) - 4.0 * h)
        write(r, u + s_main[r] * lap, h + s_side[r] * lap_h)

    def write_b(r, u, h):
        main_b[r] = u
        side_b[r] = h

    def write_a(r, u, h):
        main_a[r] = u
        side_a[r] = h

    def write_out(r, u, h):
        out[r - PASSES] = u

    for p, (main, sides, write) in enumerate((
            (main_a, side_a, write_b), (main_b, side_b, write_a), (main_a, side_a, write_out))):
        start, count = p + 1, frows + 2 * PASSES - 2 * (p + 1)
        chunk = 4 if count % 4 == 0 else 2

        def rows(n, carry):
            for j in range(chunk):
                smooth_row(start + n * chunk + j, main, sides, write)
            return carry

        lax.fori_loop(0, count // chunk, rows, 0)


def arrival_wait(target, source, sem):
    pltpu.make_async_copy(source, target, sem).wait()


def split_weights(w_copy, w_full, w_high, w_low):
    w_copy.wait()

    def one(i, carry):
        value = w_full[i]
        high = value.astype(jnp.bfloat16)
        w_high[i] = high
        w_low[i] = (value - high.astype(jnp.float32)).astype(jnp.bfloat16)
        return carry

    lax.fori_loop(0, w_full.shape[0], one, 0)


def shards(source, remap_weights, intersection_devices, intersection_rows, smoothing):
    along_x = lax.axis_size("gx")
    along_y = lax.axis_size("gy")
    devices = along_x * along_y
    frows, fanin, block = remap_weights.shape[:3]
    levels, srows = source.shape[:2]
    capacity = 2 * max(1, frows * fanin // devices)
    depth, inner = layout(along_x, along_y, capacity, srows)
    columns = along_x * inner
    x, y = lax.axis_index("gx"), lax.axis_index("gy")
    z, yi = y // inner, y % inner
    column = x * inner + yi

    def plane(table):
        table = table.reshape(along_x, depth, inner, frows, fanin)
        table = lax.dynamic_index_in_dim(table, z, 1, keepdims=False)
        return table.reshape(columns, frows * fanin)

    entries, lats = plane(intersection_devices), plane(intersection_rows)
    order = jnp.arange(frows * fanin)
    same = jnp.logical_and(entries[:, :, None] == entries[:, None, :], order[None, :] < order[:, None])
    slots = jnp.sum(same.astype(jnp.int32), axis=2)
    tiles = x * along_y + jnp.arange(depth) * inner + yi
    matched = jnp.logical_and(
        entries[:, None, None, :] == tiles[None, :, None, None],
        slots[:, None, None, :] == jnp.arange(capacity)[None, None, :, None])
    send_rows = jnp.sum(jnp.where(matched, lats[:, None, None, :], 0), axis=3).reshape(-1)
    mine = lax.dynamic_index_in_dim(entries, column, 0, keepdims=False)
    my_slots = lax.dynamic_index_in_dim(slots, column, 0, keepdims=False)
    my_y = mine % along_y
    pick = (((mine // along_y) * inner + my_y % inner) * depth + my_y // inner) * capacity + my_slots

    full = frows + 2 * PASSES
    vmem = functools.partial(pltpu.VMEM, dtype=jnp.float32)
    tile = (levels, block)
    in_vmem = pl.BlockSpec(memory_space=pltpu.VMEM)
    in_smem = pl.BlockSpec(memory_space=pltpu.SMEM)
    slots_all = columns * depth * capacity
    dma = pltpu.SemaphoreType.DMA
    field = pl.pallas_call(
        functools.partial(kernel, (along_x, along_y, depth, inner, capacity)),
        out_shape=jax.ShapeDtypeStruct((frows,) + tile, jnp.float32),
        in_specs=[in_smem, in_smem, in_vmem, pl.BlockSpec(memory_space=pl.ANY), in_vmem],
        out_specs=in_vmem,
        scratch_shapes=[
            vmem((slots_all,) + tile),
            vmem((slots_all,) + tile),
            vmem((frows, fanin * block, block)),
            pltpu.VMEM((frows, fanin * block, block), jnp.bfloat16),
            pltpu.VMEM((frows, fanin * block, block), jnp.bfloat16),
            vmem((full,) + tile), vmem((full,) + tile), vmem((full,) + tile), vmem((full,) + tile),
            vmem((full, 1, block)), vmem((full, 1, block)),
            vmem((len(DIRS), frows, block)),
            vmem((frows // PER_TILE,) + tile),
            vmem((len(DIRS), frows // PER_TILE) + tile),
            dma((columns * depth,)), dma((columns * depth,)),
            dma((2, max(1, depth - 1))), dma((2, max(1, depth - 1))),
            dma((len(DIRS),)), dma((len(DIRS),)), dma((len(DIRS),)), dma((len(DIRS),)),
            dma,
        ] + [vmem((srows,) + tile)] * (2 * (depth - 1)),
        compiler_params=pltpu.CompilerParams(
            collective_id=0, has_side_effects=True, vmem_limit_bytes=48 * 2 ** 20),
        cost_estimate=pl.CostEstimate(
            flops=6 * levels * frows * fanin * block * block, bytes_accessed=16 * 2 ** 20, transcendentals=0),
    )(send_rows, pick, source.transpose(1, 0, 2),
      remap_weights.reshape(frows, fanin * block, block), smoothing)
    return field.transpose(1, 0, 2)


def solution(mesh):
    return jax.shard_map(
        shards,
        mesh=mesh,
        in_specs=(P("lev", "gy", "gx"), P(("gx", "gy"), None, None, None), P(), P(), P("gx", "gy")),
        out_specs=P("lev", "gx", "gy"),
        check_vma=False,
    )
```

```python
import functools

import jax
import jax.numpy as jnp
from jax import lax
from jax.experimental import pallas as pl
from jax.experimental.pallas import tpu as pltpu
from jax.sharding import PartitionSpec as P

PASSES = 3
MESH = pl.DeviceIdType.MESH
DIRS = [(dx, dy) for dx in (-1, 0, 1) for dy in (-1, 0, 1) if (dx, dy) != (0, 0)]
OPPOSITE = [DIRS.index((-dx, -dy)) for dx, dy in DIRS]
LANES = 128
STRIP = 8
PER_TILE = LANES // STRIP
HALVES = 2
W_PIECES = 4
GROUP = 4


def layout(along_x, along_y, capacity, rows):
    inner = 2 if along_y % 2 == 0 else 1
    if capacity * inner * along_x > rows:
        return along_y // inner, inner
    return 1, along_y


def kernel(dims, send_rows, pick, src, weights, smooth, out, inbox_0, inbox_1, outbox, w_full, w_high, w_low,
           main_a, main_b, side_a, side_b, s_main, s_side, s_in, edge, edge_in,
           send_sem, recv_sem, chain_send, chain_recv, s_send, s_recv, h_send, h_recv, w_sem, *chunks):
    along_x, along_y, depth, inner, capacity = dims
    frows, fan = w_full.shape[0], pick.shape[0] // w_full.shape[0]
    levels, srows = src.shape[:2]
    sub = levels // HALVES
    width = LANES // HALVES
    columns = along_x * inner
    inboxes = (inbox_0, inbox_1)
    own, chain = chunks[:HALVES], chunks[HALVES:]
    ups = [chain[h * (depth - 1):(h + 1) * (depth - 1)] for h in range(HALVES)]
    downs = [chain[(HALVES + h) * (depth - 1):(HALVES + h + 1) * (depth - 1)] for h in range(HALVES)]
    x, y, lev = lax.axis_index("gx"), lax.axis_index("gy"), lax.axis_index("lev")
    z, yi = y // inner, y % inner
    column = x * inner + yi
    lane = lax.broadcasted_iota(jnp.int32, (levels, LANES), 1)
    lane_8 = lax.broadcasted_iota(jnp.int32, (sub, LANES), 1)
    tiles = frows // PER_TILE
    at = {d: k for k, d in enumerate(DIRS)}

    def column_id(c):
        return (c // inner, z * inner + c % inner, lev)

    def near(dx, dy):
        ok = jnp.logical_and(
            jnp.logical_and(x + dx >= 0, x + dx < along_x),
            jnp.logical_and(y + dy >= 0, y + dy < along_y),
        )
        return ok, (x + dx, y + dy, lev)

    barrier = pltpu.get_barrier_semaphore()

    def greet(device):
        pl.semaphore_signal(barrier, inc=1, device_id=device, device_id_type=MESH)

    def greet_column(q, carry):
        greet(column_id(lax.rem(column + q, columns)))
        return carry

    lax.fori_loop(1, columns, greet_column, 0)
    total = columns - 1
    links = [near(dx, dy) for dx, dy in DIRS]
    if depth > 1:
        links = links + [(z < depth - 1, (x, y + inner, lev)), (z > 0, (x, y - inner, lev))]
    for ok, device in links:
        total = total + ok.astype(jnp.int32)

        @pl.when(ok)
        def _():
            greet(device)

    share = frows // W_PIECES

    def w_copy(n):
        rows = pl.ds(n * share, share)
        return pltpu.make_async_copy(weights.at[rows], w_full.at[rows], w_sem.at[n])

    for n in range(W_PIECES):
        w_copy(n).start()

    def swapped(value):
        return pltpu.roll(value, width, axis=1)

    for b in range(srows // 8):
        for l in range(sub):
            low, high = src[l, 8 * b:8 * b + 8, :], src[sub + l, 8 * b:8 * b + 8, :]
            place = pl.ds(8 * b, 8)
            own[0][place, l, :] = jnp.where(lane_8 < width, low, swapped(high))
            own[1][place, l, :] = jnp.where(lane_8 < width, swapped(low), high)

    pl.semaphore_wait(barrier, total)

    def chain_copy(h, up, t):
        boxes = (ups if up else downs)[h]
        return pltpu.make_async_remote_copy(
            src_ref=own[h] if t == 0 else boxes[t - 1], dst_ref=boxes[t],
            send_sem=chain_send.at[h, 0 if up else 1, t], recv_sem=chain_recv.at[h, 0 if up else 1, t],
            device_id=(x, y + (inner if up else -inner), lev), device_id_type=MESH)

    def slot_copy(h, q, tile):
        c = lax.rem(column + q, columns)
        sem = (h * columns + q) * depth + tile
        return pltpu.make_async_remote_copy(
            src_ref=outbox.at[h, pl.ds((c * depth + tile) * capacity, capacity)],
            dst_ref=inboxes[h].at[pl.ds((column * depth + tile) * capacity, capacity)],
            send_sem=send_sem.at[sem], recv_sem=recv_sem.at[sem],
            device_id=column_id(c), device_id_type=MESH)

    def ship(h, chunk, tile):
        def block(n):
            return chunk[send_rows[n]]

        def peer(q, carry):
            base = (lax.rem(column + q, columns) * depth + tile) * capacity
            for j in range(capacity):
                outbox[h, base + j] = block(base + j)
            slot_copy(h, q, tile).start()
            return carry

        lax.fori_loop(1, columns, peer, 0)
        base = (column * depth + tile) * capacity
        for j in range(capacity):
            inboxes[h][base + j] = block(base + j)

    def start_chain(h):
        if depth > 1:
            @pl.when(z < depth - 1)
            def _():
                chain_copy(h, True, 0).start()

            @pl.when(z > 0)
            def _():
                chain_copy(h, False, 0).start()

    def pass_on(h, t):
        for up, ok, onward in ((True, z >= t + 1, z < depth - 1), (False, z + 1 + t <= depth - 1, z > 0)):
            @pl.when(ok)
            def _():
                chain_copy(h, up, t).wait_recv()
                if t + 1 < depth - 1:
                    @pl.when(onward)
                    def _():
                        chain_copy(h, up, t + 1).start()
                ship(h, (ups if up else downs)[h][t], z - 1 - t if up else z + 1 + t)

    def s_copy(k):
        ok, device = near(*DIRS[k])
        return ok, pltpu.make_async_remote_copy(
            src_ref=smooth, dst_ref=s_in.at[OPPOSITE[k]], send_sem=s_send.at[k],
            recv_sem=s_recv.at[OPPOSITE[k]], device_id=device, device_id_type=MESH)

    def h_copy(k, tile):
        dx, dy = DIRS[k]
        ok, device = near(dx, dy)
        if dy == 0:
            source = main_a.at[pl.ds(frows if dx > 0 else PASSES, PASSES)]
            target = main_a.at[pl.ds(0 if dx > 0 else frows + PASSES, PASSES)]
        else:
            source, target = edge.at[tile], edge_in.at[OPPOSITE[k], tile]
        return ok, pltpu.make_async_remote_copy(
            src_ref=source, dst_ref=target, send_sem=h_send.at[k, tile],
            recv_sem=h_recv.at[OPPOSITE[k], tile], device_id=device, device_id_type=MESH)

    def split_weights(n):
        w_copy(n).wait()

        def one(i, carry):
            for k in range(fan):
                for h in range(HALVES):
                    value = w_full[i, pl.ds(k * LANES + h * width, width), :]
                    high = value.astype(jnp.bfloat16)
                    place = pl.ds(k * width, width)
                    w_high[h, i, place, :] = high
                    w_low[h, i, place, :] = (value - high.astype(jnp.float32)).astype(jnp.bfloat16)
            return carry

        lax.fori_loop(n * share, (n + 1) * share, one, 0)

    def product(h, i):
        rows = [[], []]
        for k in range(0, fan, 2):
            even, odd = inboxes[h][pick[i * fan + k]], inboxes[h][pick[i * fan + k + 1]]
            rows[0].append(jnp.where(lane_8 < width, even, swapped(odd)))
            rows[1].append(jnp.where(lane_8 < width, swapped(even), odd))
        blocks = jnp.concatenate([jnp.concatenate(r, axis=1) for r in rows], axis=0)
        high = blocks.astype(jnp.bfloat16)
        low = (blocks - high.astype(jnp.float32)).astype(jnp.bfloat16)
        both = jnp.dot(jnp.concatenate([high, low], axis=0), w_high[h, i], preferred_element_type=jnp.float32)
        rest = jnp.dot(high, w_low[h, i], preferred_element_type=jnp.float32)
        result = both[:levels] + (both[levels:] + rest)
        if h == 0:
            main_a[PASSES + i] = result
        else:
            main_a[PASSES + i] += result

    groups = frows // GROUP

    def products(h, start, stop):
        def some(n, carry):
            for j in range(GROUP):
                product(h, n * GROUP + j)
            return carry

        lax.fori_loop(start, stop, some, 0)

    def landed(h):
        def one(n, carry):
            slot_copy(h, n // depth, lax.rem(n, depth)).wait_recv()
            return carry

        lax.fori_loop(depth, columns * depth, one, 0)

    start_chain(0)
    ship(0, own[0], z)
    for k in range(len(DIRS)):
        ok, copy = s_copy(k)

        @pl.when(ok)
        def _():
            copy.start()

    for k, (dx, dy) in enumerate(DIRS):
        ok, _ = near(dx, dy)

        @pl.when(jnp.logical_not(ok))
        def _():
            s_in[k] = jnp.zeros(s_in.shape[1:], jnp.float32)
            if dy == 0:
                main_a[pl.ds(0 if dx < 0 else frows + PASSES, PASSES)] = jnp.zeros(
                    (PASSES,) + main_a.shape[1:], jnp.float32)
            else:
                edge_in[k] = jnp.zeros(edge_in.shape[1:], jnp.float32)

    second = min(1, depth - 2)
    done = 0
    for t in range(depth - 1):
        pass_on(0, t)
        if t == second:
            start_chain(1)
        if done < W_PIECES:
            split_weights(done)
            done += 1

    ship(1, own[1], z)
    for n in range(done, W_PIECES):
        split_weights(n)

    for k in range(len(DIRS)):
        ok, copy = s_copy(k)

        @pl.when(ok)
        def _():
            copy.wait_send()
            arrival_wait(s_in.at[k], smooth, s_recv.at[k])

    row_lane = lax.broadcasted_iota(jnp.int32, (1, LANES), 1)

    def side(left, right):
        return jnp.where(row_lane < PASSES, right, jnp.where(row_lane >= LANES - PASSES, left, 0.0))

    for i in range(frows):
        s_main[PASSES + i] = smooth[i:i + 1, :]
        s_side[PASSES + i] = side(s_in[at[0, -1], i:i + 1, :], s_in[at[0, 1], i:i + 1, :])
    for i in range(PASSES):
        low, high = frows - PASSES + i, frows + PASSES + i
        s_main[i] = s_in[at[-1, 0], low:low + 1, :]
        s_side[i] = side(s_in[at[-1, -1], low:low + 1, :], s_in[at[-1, 1], low:low + 1, :])
        s_main[high] = s_in[at[1, 0], i:i + 1, :]
        s_side[high] = side(s_in[at[1, -1], i:i + 1, :], s_in[at[1, 1], i:i + 1, :])

    steps = max(1, depth - 1)
    for t in range(steps):
        if t < depth - 1:
            pass_on(1, t)
        if t == 0:
            landed(0)
        products(0, groups * t // steps, groups * (t + 1) // steps)
    landed(1)

    def send_halo(wanted):
        for k, (dx, dy) in enumerate(DIRS):
            for tile in wanted(dx, dy):
                ok, copy = h_copy(k, tile)

                @pl.when(ok)
                def _():
                    copy.start()

    def halo_tiles(dx, dy):
        if dy == 0:
            return [0]
        return list(range(tiles)) if dx == 0 else [0 if dx < 0 else tiles - 1]

    def pack(b):
        packed = jnp.zeros((levels, LANES), jnp.float32)
        for j in range(PER_TILE):
            moved = pltpu.roll(main_a[PASSES + b * PER_TILE + j], STRIP * j + STRIP // 2, axis=1)
            packed = jnp.where(lane // STRIP == j, moved, packed)
        edge[b] = packed
        send_halo(lambda dx, dy: [b] if dy != 0 and b in halo_tiles(dx, dy) else [])

    products(1, 0, 1)
    products(1, groups - 1, groups)
    send_halo(lambda dx, dy: [0] if dy == 0 else [])
    for b in range(tiles):
        products(1, max(1, b * groups // tiles), min(groups - 1, (b + 1) * groups // tiles))
        pack(b)

    def sent(n, carry):
        for h in range(HALVES):
            slot_copy(h, n // depth, lax.rem(n, depth)).wait_send()
        return carry

    lax.fori_loop(depth, columns * depth, sent, 0)
    for t in range(depth - 1):
        for h in range(HALVES):
            @pl.when(jnp.logical_and(z < depth - 1, z - t >= 0))
            def _():
                chain_copy(h, True, t).wait_send()

            @pl.when(jnp.logical_and(z > 0, z + t <= depth - 1))
            def _():
                chain_copy(h, False, t).wait_send()

    for k, (dx, dy) in enumerate(DIRS):
        for tile in halo_tiles(dx, dy):
            ok, copy = h_copy(k, tile)

            @pl.when(ok)
            def _():
                copy.wait_send()

        for tile in halo_tiles(-dx, -dy):
            @pl.when(near(dx, dy)[0])
            def _():
                if dy == 0:
                    rows = main_a.at[pl.ds(0 if dx < 0 else frows + PASSES, PASSES)]
                    arrival_wait(rows, rows, h_recv.at[k, tile])
                else:
                    arrival_wait(edge_in.at[k, tile], edge.at[tile], h_recv.at[k, tile])

    inside = jnp.logical_or(lane < PASSES, lane >= LANES - PASSES)

    def unpack(row, tile, place, left, right):
        merged = jnp.where(lax.rem(lane, STRIP) < STRIP // 2, edge_in[left, tile], edge_in[right, tile])
        moved = pltpu.roll(merged, (2 * LANES - STRIP * place - STRIP // 2) % LANES, axis=1)
        side_a[row] = jnp.where(inside, moved, 0.0)

    for i in range(frows):
        unpack(PASSES + i, i // PER_TILE, i % PER_TILE, at[0, -1], at[0, 1])
    for i in range(PASSES):
        far = frows - PASSES + i
        unpack(i, far // PER_TILE, far % PER_TILE, at[-1, -1], at[-1, 1])
        unpack(frows + PASSES + i, 0, i, at[1, -1], at[1, 1])

    first, last = lane == 0, lane == LANES - 1

    def smooth_row(r, main, sides, write):
        u, h = main[r], sides[r]
        u_up, u_down = pltpu.roll(u, 1, axis=1), pltpu.roll(u, LANES - 1, axis=1)
        h_up, h_down = pltpu.roll(h, 1, axis=1), pltpu.roll(h, LANES - 1, axis=1)
        lap = (main[r + 1] + main[r - 1] + jnp.where(last, h_down, u_down)
               + jnp.where(first, h_up, u_up) - 4.0 * u)
        lap_h = (sides[r + 1] + sides[r - 1] + jnp.where(last, u_down, h_down)
                 + jnp.where(first, u_up, h_up) - 4.0 * h)
        write(r, u + s_main[r] * lap, h + s_side[r] * lap_h)

    def write_b(r, u, h):
        main_b[r] = u
        side_b[r] = h

    def write_a(r, u, h):
        main_a[r] = u
        side_a[r] = h

    def write_out(r, u, h):
        out[pl.ds(r - PASSES, levels, stride=frows), :] = u

    for p, (main, sides, write) in enumerate((
            (main_a, side_a, write_b), (main_b, side_b, write_a), (main_a, side_a, write_out))):
        start, count = p + 1, frows + 2 * PASSES - 2 * (p + 1)
        chunk = 4 if count % 4 == 0 else 2

        def rows(n, carry):
            for j in range(chunk):
                smooth_row(start + n * chunk + j, main, sides, write)
            return carry

        lax.fori_loop(0, count // chunk, rows, 0)


def arrival_wait(target, source, sem):
    pltpu.make_async_copy(source, target, sem).wait()


def shards(source, remap_weights, intersection_devices, intersection_rows, smoothing):
    along_x = lax.axis_size("gx")
    along_y = lax.axis_size("gy")
    devices = along_x * along_y
    frows, fanin, block = remap_weights.shape[:3]
    levels, srows = source.shape[:2]
    capacity = 2 * max(1, frows * fanin // devices)
    depth, inner = layout(along_x, along_y, capacity, srows)
    columns = along_x * inner
    x, y = lax.axis_index("gx"), lax.axis_index("gy")
    z, yi = y // inner, y % inner
    column = x * inner + yi

    codes = intersection_devices * srows + intersection_rows
    plane = jnp.concatenate([
        lax.dynamic_slice_in_dim(codes, (i * along_y + z * inner) * frows, inner * frows, 0) for i in range(along_x)])
    plane = plane.reshape(columns, frows * fanin)
    entries, lats = plane // srows, plane % srows
    order = jnp.arange(frows * fanin)
    same = jnp.logical_and(entries[:, :, None] == entries[:, None, :], order[None, :] < order[:, None])
    slots = jnp.sum(same.astype(jnp.int32), axis=2)
    tiles = x * along_y + jnp.arange(depth) * inner + yi
    matched = jnp.logical_and(
        entries[:, None, None, :] == tiles[None, :, None, None],
        slots[:, None, None, :] == jnp.arange(capacity)[None, None, :, None])
    send_rows = jnp.sum(jnp.where(matched, lats[:, None, None, :], 0), axis=3).reshape(-1)
    mine = lax.dynamic_index_in_dim(entries, column, 0, keepdims=False)
    my_slots = lax.dynamic_index_in_dim(slots, column, 0, keepdims=False)
    my_y = mine % along_y
    pick = (((mine // along_y) * inner + my_y % inner) * depth + my_y // inner) * capacity + my_slots

    full = frows + 2 * PASSES
    sub = levels // HALVES
    vmem = functools.partial(pltpu.VMEM, dtype=jnp.float32)
    tile = (levels, block)
    in_vmem = pl.BlockSpec(memory_space=pltpu.VMEM)
    in_smem = pl.BlockSpec(memory_space=pltpu.SMEM)
    slots_all = columns * depth * capacity
    dma = pltpu.SemaphoreType.DMA
    sides = len(DIRS)
    edges = frows // PER_TILE
    halves = pltpu.VMEM((HALVES, frows, fanin * block // HALVES, block), jnp.bfloat16)
    field = pl.pallas_call(
        functools.partial(kernel, (along_x, along_y, depth, inner, capacity)),
        out_shape=jax.ShapeDtypeStruct((levels * frows, block), jnp.float32),
        in_specs=[in_smem, in_smem, in_vmem, pl.BlockSpec(memory_space=pl.ANY), in_vmem],
        out_specs=in_vmem,
        scratch_shapes=[
            vmem((slots_all, sub, block)), vmem((slots_all, sub, block)),
            vmem((HALVES, slots_all, sub, block)),
            vmem((frows, fanin * block, block)),
            halves, halves,
            vmem((full,) + tile), vmem((full,) + tile), vmem((full,) + tile), vmem((full,) + tile),
            vmem((full, 1, block)), vmem((full, 1, block)),
            vmem((sides, frows, block)),
            vmem((edges,) + tile),
            vmem((sides, edges) + tile),
            dma((HALVES * columns * depth,)), dma((HALVES * columns * depth,)),
            dma((HALVES, 2, max(1, depth - 1))), dma((HALVES, 2, max(1, depth - 1))),
            dma((sides,)), dma((sides,)), dma((sides, edges)), dma((sides, edges)),
            dma((W_PIECES,)),
        ] + [vmem((srows, sub, block))] * (HALVES + 2 * HALVES * (depth - 1)),
        compiler_params=pltpu.CompilerParams(
            collective_id=0, has_side_effects=True, vmem_limit_bytes=48 * 2 ** 20),
        cost_estimate=pl.CostEstimate(
            flops=6 * levels * frows * fanin * block * block, bytes_accessed=16 * 2 ** 20, transcendentals=0),
    )(send_rows, pick, source, remap_weights.reshape(frows, fanin * block, block), smoothing)
    return field.reshape(levels, frows, block)


def solution(mesh):
    return jax.shard_map(
        shards,
        mesh=mesh,
        in_specs=(P("lev", "gy", "gx"), P(("gx", "gy"), None, None, None), P(), P(), P("gx", "gy")),
        out_specs=P("lev", "gx", "gy"),
        check_vma=False,
    )
```

```python
import functools

import jax
import jax.numpy as jnp
from jax import lax
from jax.experimental import pallas as pl
from jax.experimental.pallas import tpu as pltpu
from jax.sharding import PartitionSpec as P

PASSES = 3
MESH = pl.DeviceIdType.MESH
DIRS = [(dx, dy) for dx in (-1, 0, 1) for dy in (-1, 0, 1) if (dx, dy) != (0, 0)]
OPPOSITE = [DIRS.index((-dx, -dy)) for dx, dy in DIRS]
LANES = 128
STRIP = 8
PER_TILE = LANES // STRIP
HALVES = 2
W_PIECES = 4
GROUP = 8


def layout(along_x, along_y, capacity, rows):
    inner = 2 if along_y % 2 == 0 else 1
    if capacity * inner * along_x > rows:
        return along_y // inner, inner
    return 1, along_y


def kernel(dims, devices_in, rows_in, src_in, weights, smooth_in, out, devices, lat, src, smooth,
           table_v, pick_v, table, pick, inbox_0, inbox_1, outbox, w_full, w_high, w_low,
           main_a, main_b, side_a, side_b, s_main, s_side, s_in, edge, edge_in,
           send_sem, recv_sem, chain_send, chain_recv, s_send, s_recv, h_send, h_recv, w_sem, in_sem, *chunks):
    along_x, along_y, depth, inner, capacity = dims
    frows, fan = w_full.shape[0], devices.shape[0]
    levels, srows = src.shape[:2]
    sub = levels // HALVES
    width = LANES // HALVES
    columns = along_x * inner
    inboxes = (inbox_0, inbox_1)
    own, chain = chunks[:HALVES], chunks[HALVES:]
    ups = [chain[h * (depth - 1):(h + 1) * (depth - 1)] for h in range(HALVES)]
    downs = [chain[(HALVES + h) * (depth - 1):(HALVES + h + 1) * (depth - 1)] for h in range(HALVES)]
    x, y, lev = lax.axis_index("gx"), lax.axis_index("gy"), lax.axis_index("lev")
    z, yi = y // inner, y % inner
    column = x * inner + yi
    lane = lax.broadcasted_iota(jnp.int32, (levels, LANES), 1)
    lane_8 = lax.broadcasted_iota(jnp.int32, (sub, LANES), 1)
    tiles = frows // PER_TILE
    at = {d: k for k, d in enumerate(DIRS)}

    def column_id(c):
        return (c // inner, z * inner + c % inner, lev)

    def near(dx, dy):
        ok = jnp.logical_and(
            jnp.logical_and(x + dx >= 0, x + dx < along_x),
            jnp.logical_and(y + dy >= 0, y + dy < along_y),
        )
        return ok, (x + dx, y + dy, lev)

    loads = [pltpu.make_async_copy(a, b, in_sem.at[n]) for n, (a, b) in enumerate((
        (src_in, src), (devices_in, devices), (rows_in, lat), (smooth_in, smooth)))]
    for load in loads:
        load.start()

    barrier = pltpu.get_barrier_semaphore()

    def greet(device):
        pl.semaphore_signal(barrier, inc=1, device_id=device, device_id_type=MESH)

    def greet_column(q, carry):
        greet(column_id(lax.rem(column + q, columns)))
        return carry

    lax.fori_loop(1, columns, greet_column, 0)
    total = columns - 1
    links = [near(dx, dy) for dx, dy in DIRS]
    if depth > 1:
        links = links + [(z < depth - 1, (x, y + inner, lev)), (z > 0, (x, y - inner, lev))]
    for ok, device in links:
        total = total + ok.astype(jnp.int32)

        @pl.when(ok)
        def _():
            greet(device)

    share = frows // W_PIECES

    def w_copy(n):
        rows = pl.ds(n * share, share)
        return pltpu.make_async_copy(weights.at[rows], w_full.at[rows], w_sem.at[n])

    for n in range(W_PIECES):
        w_copy(n).start()

    for load in loads[1:]:
        load.wait()
    me = x * along_y + y
    wide = (LANES, LANES)
    from_lane = lax.broadcasted_iota(jnp.int32, wide, 0)
    to_lane = lax.broadcasted_iota(jnp.int32, wide, 1)
    together = from_lane // frows == to_lane // frows
    group_ones = jnp.where(together, 1.0, 0.0).astype(jnp.bfloat16)
    earlier = jnp.where(jnp.logical_and(together, from_lane < to_lane), 1.0, 0.0).astype(jnp.bfloat16)

    def count(hits, matrix):
        return jnp.dot(hits.astype(jnp.bfloat16), matrix, preferred_element_type=jnp.float32)

    def ranks(hits):
        found, before = [], None
        for k in range(fan):
            within = count(hits[k], earlier)
            found.append(within if before is None else within + before)
            if k + 1 < fan:
                whole = count(hits[k], group_ones)
                before = whole if before is None else before + whole
        return found

    groups_in_tile = LANES // frows
    slot = lax.broadcasted_iota(jnp.int32, (capacity, LANES), 0).astype(jnp.float32)
    mine = lax.broadcasted_iota(jnp.int32, (max(8, depth), LANES), 0) * inner + x * along_y + yi
    rows_of = jnp.zeros((depth * capacity, LANES), jnp.float32)
    for n in range(devices.shape[1] // LANES):
        span = slice(n * LANES, (n + 1) * LANES)
        hits = [jnp.where(devices[k:k + 1, span] == mine, 1.0, 0.0) for k in range(fan)]
        found = ranks(hits)
        parts = []
        for t in range(depth):
            part = jnp.zeros((capacity, LANES), jnp.float32)
            for k in range(fan):
                rank = jnp.where(hits[k][t:t + 1] > 0.5, found[k][t:t + 1], -1.0)
                part = part + jnp.where(rank == slot, lat[k:k + 1, span].astype(jnp.float32), 0.0)
            parts.append(part)
        gather = jnp.where(from_lane // frows + n * groups_in_tile == to_lane, 1.0, 0.0).astype(jnp.bfloat16)
        rows_of = rows_of + count(jnp.concatenate(parts, axis=0) if depth > 1 else parts[0], gather)
    table_v[...] = jnp.clip(rows_of.astype(jnp.int32), 0, srows - 1)

    span = pl.ds(pl.multiple_of(me // groups_in_tile * LANES, LANES), LANES)
    every = lax.broadcasted_iota(jnp.int32, (along_x * along_y, LANES), 0)
    named = [devices[k:k + 1, span] for k in range(fan)]
    hits = [jnp.where(named[k] == every, 1.0, 0.0) for k in range(fan)]
    found = ranks(hits)
    for k in range(fan):
        rank = jnp.sum(hits[k] * found[k], axis=0, keepdims=True).astype(jnp.int32)
        tile_y = lax.rem(named[k], along_y)
        base = (named[k] // along_y * inner + lax.rem(tile_y, inner)) * depth + tile_y // inner
        pick_v[k:k + 1, :] = jnp.clip(base * capacity + rank, 0, columns * depth * capacity - 1)
    tables = [pltpu.make_async_copy(a, b, in_sem.at[4 + n]) for n, (a, b) in enumerate((
        (table_v, table), (pick_v, pick)))]
    for copy in tables:
        copy.start()
    my_lane = lax.rem(me, groups_in_tile) * frows
    loads[0].wait()

    def swapped(value):
        return pltpu.roll(value, width, axis=1)

    for b in range(srows // 8):
        for l in range(sub):
            low, high = src[l, 8 * b:8 * b + 8, :], src[sub + l, 8 * b:8 * b + 8, :]
            place = pl.ds(8 * b, 8)
            own[0][place, l, :] = jnp.where(lane_8 < width, low, swapped(high))
            own[1][place, l, :] = jnp.where(lane_8 < width, swapped(low), high)

    for copy in tables:
        copy.wait()
    pl.semaphore_wait(barrier, total)

    def chain_copy(h, up, t):
        boxes = (ups if up else downs)[h]
        return pltpu.make_async_remote_copy(
            src_ref=own[h] if t == 0 else boxes[t - 1], dst_ref=boxes[t],
            send_sem=chain_send.at[h, 0 if up else 1, t], recv_sem=chain_recv.at[h, 0 if up else 1, t],
            device_id=(x, y + (inner if up else -inner), lev), device_id_type=MESH)

    def slot_copy(h, q, tile):
        c = lax.rem(column + q, columns)
        sem = (h * columns + q) * depth + tile
        return pltpu.make_async_remote_copy(
            src_ref=outbox.at[h, pl.ds((c * depth + tile) * capacity, capacity)],
            dst_ref=inboxes[h].at[pl.ds((column * depth + tile) * capacity, capacity)],
            send_sem=send_sem.at[sem], recv_sem=recv_sem.at[sem],
            device_id=column_id(c), device_id_type=MESH)

    def ship(h, chunk, tile):
        def fill(c, write):
            owner = c // inner * along_y + z * inner + lax.rem(c, inner)
            for j in range(capacity):
                write((c * depth + tile) * capacity + j, chunk[table[tile * capacity + j, owner]])

        def to_outbox(n, value):
            outbox[h, n] = value

        def to_inbox(n, value):
            inboxes[h][n] = value

        def peer(q, carry):
            fill(lax.rem(column + q, columns), to_outbox)
            slot_copy(h, q, tile).start()
            return carry

        lax.fori_loop(1, columns, peer, 0)
        fill(column, to_inbox)

    def start_chain(h):
        if depth > 1:
            @pl.when(z < depth - 1)
            def _():
                chain_copy(h, True, 0).start()

            @pl.when(z > 0)
            def _():
                chain_copy(h, False, 0).start()

    def pass_on(h, t):
        for up, ok, onward in ((True, z >= t + 1, z < depth - 1), (False, z + 1 + t <= depth - 1, z > 0)):
            @pl.when(ok)
            def _():
                chain_copy(h, up, t).wait_recv()
                if t + 1 < depth - 1:
                    @pl.when(onward)
                    def _():
                        chain_copy(h, up, t + 1).start()
                ship(h, (ups if up else downs)[h][t], z - 1 - t if up else z + 1 + t)

    def s_copy(k):
        ok, device = near(*DIRS[k])
        return ok, pltpu.make_async_remote_copy(
            src_ref=smooth, dst_ref=s_in.at[OPPOSITE[k]], send_sem=s_send.at[k],
            recv_sem=s_recv.at[OPPOSITE[k]], device_id=device, device_id_type=MESH)

    def h_copy(k, tile):
        dx, dy = DIRS[k]
        ok, device = near(dx, dy)
        if dy == 0:
            source = main_a.at[pl.ds(frows if dx > 0 else PASSES, PASSES)]
            target = main_a.at[pl.ds(0 if dx > 0 else frows + PASSES, PASSES)]
        else:
            source, target = edge.at[tile], edge_in.at[OPPOSITE[k], tile]
        return ok, pltpu.make_async_remote_copy(
            src_ref=source, dst_ref=target, send_sem=h_send.at[k, tile],
            recv_sem=h_recv.at[OPPOSITE[k], tile], device_id=device, device_id_type=MESH)

    def split_weights(n):
        w_copy(n).wait()

        def one(i, carry):
            for k in range(fan):
                for h in range(HALVES):
                    value = w_full[i, pl.ds(k * LANES + h * width, width), :]
                    high = value.astype(jnp.bfloat16)
                    place = pl.ds(k * width, width)
                    w_high[h, i, place, :] = high
                    w_low[h, i, place, :] = (value - high.astype(jnp.float32)).astype(jnp.bfloat16)
            return carry

        lax.fori_loop(n * share, (n + 1) * share, one, 0)

    def product(h, i):
        rows = [[], []]
        for k in range(0, fan, 2):
            even, odd = (inboxes[h][pick[k + j, my_lane + i]] for j in range(2))
            rows[0].append(jnp.where(lane_8 < width, even, swapped(odd)))
            rows[1].append(jnp.where(lane_8 < width, swapped(even), odd))
        blocks = jnp.concatenate([jnp.concatenate(r, axis=1) for r in rows], axis=0)
        high = blocks.astype(jnp.bfloat16)
        low = (blocks - high.astype(jnp.float32)).astype(jnp.bfloat16)
        both = jnp.dot(jnp.concatenate([high, low], axis=0), w_high[h, i], preferred_element_type=jnp.float32)
        rest = jnp.dot(high, w_low[h, i], preferred_element_type=jnp.float32)
        result = both[:levels] + (both[levels:] + rest)
        if h == 0:
            main_a[PASSES + i] = result
        else:
            main_a[PASSES + i] += result

    groups = frows // GROUP

    def products(h, start, stop):
        def some(n, carry):
            for j in range(GROUP):
                product(h, n * GROUP + j)
            return carry

        lax.fori_loop(start, stop, some, 0)

    def landed(h):
        def one(n, carry):
            slot_copy(h, n // depth, lax.rem(n, depth)).wait_recv()
            return carry

        lax.fori_loop(depth, columns * depth, one, 0)

    start_chain(0)
    ship(0, own[0], z)
    ship(1, own[1], z)
    for k in range(len(DIRS)):
        ok, copy = s_copy(k)

        @pl.when(ok)
        def _():
            copy.start()

    for k, (dx, dy) in enumerate(DIRS):
        ok, _ = near(dx, dy)

        @pl.when(jnp.logical_not(ok))
        def _():
            s_in[k] = jnp.zeros(s_in.shape[1:], jnp.float32)
            if dy == 0:
                main_a[pl.ds(0 if dx < 0 else frows + PASSES, PASSES)] = jnp.zeros(
                    (PASSES,) + main_a.shape[1:], jnp.float32)
            else:
                edge_in[k] = jnp.zeros(edge_in.shape[1:], jnp.float32)

    done = 0
    events = sorted((t + 1.5 * h, h, t) for h in range(HALVES) for t in range(depth - 1))
    for n, (_, h, t) in enumerate(events):
        pass_on(h, t)
        if n == 0:
            start_chain(1)
        if done < W_PIECES:
            split_weights(done)
            done += 1
    for n in range(done, W_PIECES):
        split_weights(n)

    for k in range(len(DIRS)):
        ok, copy = s_copy(k)

        @pl.when(ok)
        def _():
            copy.wait_send()
            arrival_wait(s_in.at[k], smooth, s_recv.at[k])

    row_lane = lax.broadcasted_iota(jnp.int32, (1, LANES), 1)

    def side(left, right):
        return jnp.where(row_lane < PASSES, right, jnp.where(row_lane >= LANES - PASSES, left, 0.0))

    for i in range(frows):
        s_main[PASSES + i] = smooth[i:i + 1, :]
        s_side[PASSES + i] = side(s_in[at[0, -1], i:i + 1, :], s_in[at[0, 1], i:i + 1, :])
    for i in range(PASSES):
        low, high = frows - PASSES + i, frows + PASSES + i
        s_main[i] = s_in[at[-1, 0], low:low + 1, :]
        s_side[i] = side(s_in[at[-1, -1], low:low + 1, :], s_in[at[-1, 1], low:low + 1, :])
        s_main[high] = s_in[at[1, 0], i:i + 1, :]
        s_side[high] = side(s_in[at[1, -1], i:i + 1, :], s_in[at[1, 1], i:i + 1, :])

    landed(0)
    products(0, 0, groups)
    landed(1)

    def send_halo(wanted):
        for k, (dx, dy) in enumerate(DIRS):
            for tile in wanted(dx, dy):
                ok, copy = h_copy(k, tile)

                @pl.when(ok)
                def _():
                    copy.start()

    def halo_tiles(dx, dy):
        if dy == 0:
            return [0]
        return list(range(tiles)) if dx == 0 else [0 if dx < 0 else tiles - 1]

    def pack(b):
        packed = jnp.zeros((levels, LANES), jnp.float32)
        for j in range(PER_TILE):
            moved = pltpu.roll(main_a[PASSES + b * PER_TILE + j], STRIP * j + STRIP // 2, axis=1)
            packed = jnp.where(lane // STRIP == j, moved, packed)
        edge[b] = packed
        send_halo(lambda dx, dy: [b] if dy != 0 and b in halo_tiles(dx, dy) else [])

    products(1, 0, 1)
    products(1, groups - 1, groups)
    send_halo(lambda dx, dy: [0] if dy == 0 else [])
    for b in range(tiles):
        products(1, max(1, b * groups // tiles), min(groups - 1, (b + 1) * groups // tiles))
        pack(b)

    def sent(n, carry):
        for h in range(HALVES):
            slot_copy(h, n // depth, lax.rem(n, depth)).wait_send()
        return carry

    lax.fori_loop(depth, columns * depth, sent, 0)
    for t in range(depth - 1):
        for h in range(HALVES):
            @pl.when(jnp.logical_and(z < depth - 1, z - t >= 0))
            def _():
                chain_copy(h, True, t).wait_send()

            @pl.when(jnp.logical_and(z > 0, z + t <= depth - 1))
            def _():
                chain_copy(h, False, t).wait_send()

    for k, (dx, dy) in enumerate(DIRS):
        for tile in halo_tiles(dx, dy):
            ok, copy = h_copy(k, tile)

            @pl.when(ok)
            def _():
                copy.wait_send()

        for tile in halo_tiles(-dx, -dy):
            @pl.when(near(dx, dy)[0])
            def _():
                if dy == 0:
                    rows = main_a.at[pl.ds(0 if dx < 0 else frows + PASSES, PASSES)]
                    arrival_wait(rows, rows, h_recv.at[k, tile])
                else:
                    arrival_wait(edge_in.at[k, tile], edge.at[tile], h_recv.at[k, tile])

    inside = jnp.logical_or(lane < PASSES, lane >= LANES - PASSES)

    def unpack(row, tile, place, left, right):
        merged = jnp.where(lax.rem(lane, STRIP) < STRIP // 2, edge_in[left, tile], edge_in[right, tile])
        moved = pltpu.roll(merged, (2 * LANES - STRIP * place - STRIP // 2) % LANES, axis=1)
        side_a[row] = jnp.where(inside, moved, 0.0)

    for i in range(frows):
        unpack(PASSES + i, i // PER_TILE, i % PER_TILE, at[0, -1], at[0, 1])
    for i in range(PASSES):
        far = frows - PASSES + i
        unpack(i, far // PER_TILE, far % PER_TILE, at[-1, -1], at[-1, 1])
        unpack(frows + PASSES + i, 0, i, at[1, -1], at[1, 1])

    first, last = lane == 0, lane == LANES - 1

    def smooth_row(r, main, sides, write):
        u, h = main[r], sides[r]
        u_up, u_down = pltpu.roll(u, 1, axis=1), pltpu.roll(u, LANES - 1, axis=1)
        h_up, h_down = pltpu.roll(h, 1, axis=1), pltpu.roll(h, LANES - 1, axis=1)
        lap = (main[r + 1] + main[r - 1] + jnp.where(last, h_down, u_down)
               + jnp.where(first, h_up, u_up) - 4.0 * u)
        lap_h = (sides[r + 1] + sides[r - 1] + jnp.where(last, u_down, h_down)
                 + jnp.where(first, u_up, h_up) - 4.0 * h)
        write(r, u + s_main[r] * lap, h + s_side[r] * lap_h)

    def write_b(r, u, h):
        main_b[r] = u
        side_b[r] = h

    def write_a(r, u, h):
        main_a[r] = u
        side_a[r] = h

    def write_out(r, u, h):
        out[pl.ds(r - PASSES, levels, stride=frows), :] = u

    for p, (main, sides, write) in enumerate((
            (main_a, side_a, write_b), (main_b, side_b, write_a), (main_a, side_a, write_out))):
        start, count = p + 1, frows + 2 * PASSES - 2 * (p + 1)
        chunk = next(n for n in (12, 17, 16, 2, 1) if count % n == 0)

        def rows(n, carry):
            for j in range(chunk):
                smooth_row(start + n * chunk + j, main, sides, write)
            return carry

        lax.fori_loop(0, count // chunk, rows, 0)


def arrival_wait(target, source, sem):
    pltpu.make_async_copy(source, target, sem).wait()


def shards(source, remap_weights, intersection_devices, intersection_rows, smoothing):
    along_x = lax.axis_size("gx")
    along_y = lax.axis_size("gy")
    devices = along_x * along_y
    frows, fanin, block = remap_weights.shape[:3]
    levels, srows = source.shape[:2]
    capacity = 2 * max(1, frows * fanin // devices)
    depth, inner = layout(along_x, along_y, capacity, srows)
    columns = along_x * inner
    full = frows + 2 * PASSES
    sub = levels // HALVES
    vmem = functools.partial(pltpu.VMEM, dtype=jnp.float32)
    tile = (levels, block)
    in_vmem = pl.BlockSpec(memory_space=pltpu.VMEM)
    anywhere = pl.BlockSpec(memory_space=pl.ANY)
    entries = (fanin, intersection_devices.shape[0])
    tables = ((depth * capacity, block), (fanin, block))
    slots_all = columns * depth * capacity
    dma = pltpu.SemaphoreType.DMA
    sides = len(DIRS)
    edges = frows // PER_TILE
    halves = pltpu.VMEM((HALVES, frows, fanin * block // HALVES, block), jnp.bfloat16)
    field = pl.pallas_call(
        functools.partial(kernel, (along_x, along_y, depth, inner, capacity)),
        out_shape=jax.ShapeDtypeStruct((levels * frows, block), jnp.float32),
        in_specs=[anywhere] * 5,
        out_specs=in_vmem,
        scratch_shapes=[
            pltpu.VMEM(entries, jnp.int32), pltpu.VMEM(entries, jnp.int32),
            vmem((levels, srows, block)), vmem((frows, block)),
            *[pltpu.VMEM(shape, jnp.int32) for shape in tables],
            *[pltpu.SMEM(shape, jnp.int32) for shape in tables],
            vmem((slots_all, sub, block)), vmem((slots_all, sub, block)),
            vmem((HALVES, slots_all, sub, block)),
            vmem((frows, fanin * block, block)),
            halves, halves,
            vmem((full,) + tile), vmem((full,) + tile), vmem((full,) + tile), vmem((full,) + tile),
            vmem((full, 1, block)), vmem((full, 1, block)),
            vmem((sides, frows, block)),
            vmem((edges,) + tile),
            vmem((sides, edges) + tile),
            dma((HALVES * columns * depth,)), dma((HALVES * columns * depth,)),
            dma((HALVES, 2, max(1, depth - 1))), dma((HALVES, 2, max(1, depth - 1))),
            dma((sides,)), dma((sides,)), dma((sides, edges)), dma((sides, edges)),
            dma((W_PIECES,)), dma((6,)),
        ] + [vmem((srows, sub, block))] * (HALVES + 2 * HALVES * (depth - 1)),
        compiler_params=pltpu.CompilerParams(
            collective_id=0, has_side_effects=True, vmem_limit_bytes=56 * 2 ** 20),
        cost_estimate=pl.CostEstimate(
            flops=6 * levels * frows * fanin * block * block, bytes_accessed=16 * 2 ** 20, transcendentals=0),
    )(intersection_devices.T, intersection_rows.T, source, remap_weights.reshape(frows, fanin * block, block), smoothing)
    return field.reshape(levels, frows, block)


def solution(mesh):
    return jax.shard_map(
        shards,
        mesh=mesh,
        in_specs=(P("lev", "gy", "gx"), P(("gx", "gy"), None, None, None), P(), P(), P("gx", "gy")),
        out_specs=P("lev", "gx", "gy"),
        check_vma=False,
    )
```

```python
import functools

import jax
import jax.numpy as jnp
from jax import lax
from jax.experimental import pallas as pl
from jax.experimental.pallas import tpu as pltpu
from jax.sharding import PartitionSpec as P

PASSES = 3
MESH = pl.DeviceIdType.MESH
DIRS = [(dx, dy) for dx in (-1, 0, 1) for dy in (-1, 0, 1) if (dx, dy) != (0, 0)]
OPPOSITE = [DIRS.index((-dx, -dy)) for dx, dy in DIRS]
LANES = 128
STRIP = 8
PER_TILE = LANES // STRIP
HALVES = 2
W_PIECES = 4
GROUP = 8


def layout(along_x, along_y, capacity, rows):
    inner = 2 if along_y % 2 == 0 else 1
    if capacity * inner * along_x > rows:
        return along_y // inner, inner
    return 1, along_y


def kernel(dims, devices_in, rows_in, src_in, weights, smooth_in, out, change, devices, lat, src, smooth,
           table_v, pick_v, table, pick, inbox_0, inbox_1, outbox, w_full, w_high, w_low,
           main_a, main_b, side_a, side_b, s_main, s_side, s_in, edge, edge_in,
           send_sem, recv_sem, chain_send, chain_recv, s_send, s_recv, h_send, h_recv, w_sem, in_sem, *chunks):
    along_x, along_y, depth, inner, capacity = dims
    frows, fan = w_full.shape[0], devices.shape[0]
    levels, srows = src.shape[:2]
    sub = levels // HALVES
    width = LANES // HALVES
    columns = along_x * inner
    inboxes = (inbox_0, inbox_1)
    own, chain = chunks[:HALVES], chunks[HALVES:]
    ups = [chain[h * (depth - 1):(h + 1) * (depth - 1)] for h in range(HALVES)]
    downs = [chain[(HALVES + h) * (depth - 1):(HALVES + h + 1) * (depth - 1)] for h in range(HALVES)]
    x, y, lev = lax.axis_index("gx"), lax.axis_index("gy"), lax.axis_index("lev")
    z, yi = y // inner, y % inner
    column = x * inner + yi
    lane = lax.broadcasted_iota(jnp.int32, (levels, LANES), 1)
    lane_8 = lax.broadcasted_iota(jnp.int32, (sub, LANES), 1)
    tiles = frows // PER_TILE
    at = {d: k for k, d in enumerate(DIRS)}

    def column_id(c):
        return (c // inner, z * inner + c % inner, lev)

    def near(dx, dy):
        ok = jnp.logical_and(
            jnp.logical_and(x + dx >= 0, x + dx < along_x),
            jnp.logical_and(y + dy >= 0, y + dy < along_y),
        )
        return ok, (x + dx, y + dy, lev)

    loads = [pltpu.make_async_copy(a, b, in_sem.at[n]) for n, (a, b) in enumerate((
        (src_in, src), (devices_in, devices), (rows_in, lat), (smooth_in, smooth)))]
    for load in loads:
        load.start()

    barrier = pltpu.get_barrier_semaphore()

    def greet(device):
        pl.semaphore_signal(barrier, inc=1, device_id=device, device_id_type=MESH)

    def greet_column(q, carry):
        greet(column_id(lax.rem(column + q, columns)))
        return carry

    lax.fori_loop(1, columns, greet_column, 0)
    total = columns - 1
    links = [near(dx, dy) for dx, dy in DIRS]
    if depth > 1:
        links = links + [(z < depth - 1, (x, y + inner, lev)), (z > 0, (x, y - inner, lev))]
    for ok, device in links:
        total = total + ok.astype(jnp.int32)

        @pl.when(ok)
        def _():
            greet(device)

    share = frows // W_PIECES

    def w_copy(n):
        rows = pl.ds(n * share, share)
        return pltpu.make_async_copy(weights.at[rows], w_full.at[rows], w_sem.at[n])

    for n in range(W_PIECES):
        w_copy(n).start()

    for load in loads[1:]:
        load.wait()
    me = x * along_y + y
    wide = (LANES, LANES)
    from_lane = lax.broadcasted_iota(jnp.int32, wide, 0)
    to_lane = lax.broadcasted_iota(jnp.int32, wide, 1)
    together = from_lane // frows == to_lane // frows
    group_ones = jnp.where(together, 1.0, 0.0).astype(jnp.bfloat16)
    earlier = jnp.where(jnp.logical_and(together, from_lane < to_lane), 1.0, 0.0).astype(jnp.bfloat16)

    def count(hits, matrix):
        return jnp.dot(hits.astype(jnp.bfloat16), matrix, preferred_element_type=jnp.float32)

    def ranks(hits):
        found, before = [], None
        for k in range(fan):
            within = count(hits[k], earlier)
            found.append(within if before is None else within + before)
            if k + 1 < fan:
                whole = count(hits[k], group_ones)
                before = whole if before is None else before + whole
        return found

    groups_in_tile = LANES // frows
    slot = lax.broadcasted_iota(jnp.int32, (capacity, LANES), 0).astype(jnp.float32)
    mine = lax.broadcasted_iota(jnp.int32, (max(8, depth), LANES), 0) * inner + x * along_y + yi
    rows_of = jnp.zeros(table_v.shape, jnp.float32)
    spare = table_v.shape[1] - depth * capacity
    for n in range(devices.shape[1] // LANES):
        span = slice(n * LANES, (n + 1) * LANES)
        hits = [jnp.where(devices[k:k + 1, span] == mine, 1.0, 0.0) for k in range(fan)]
        found = ranks(hits)
        parts = []
        for t in range(depth):
            part = jnp.zeros((capacity, LANES), jnp.float32)
            for k in range(fan):
                rank = jnp.where(hits[k][t:t + 1] > 0.5, found[k][t:t + 1], -1.0)
                part = part + jnp.where(rank == slot, lat[k:k + 1, span].astype(jnp.float32), 0.0)
            parts.append(part)
        if spare:
            parts.append(jnp.zeros((spare, LANES), jnp.float32))
        owner = lax.broadcasted_iota(jnp.int32, (table_v.shape[0], LANES), 0)
        lane_of = lax.broadcasted_iota(jnp.int32, (table_v.shape[0], LANES), 1)
        gather = jnp.where(lane_of // frows + n * groups_in_tile == owner, 1.0, 0.0).astype(jnp.bfloat16)
        rows_of = rows_of + lax.dot_general(
            gather, jnp.concatenate(parts, axis=0).astype(jnp.bfloat16), (((1,), (1,)), ((), ())),
            preferred_element_type=jnp.float32)
    table_v[...] = jnp.clip(rows_of.astype(jnp.int32), 0, srows - 1)

    table_copy = pltpu.make_async_copy(table_v, table, in_sem.at[4])
    table_copy.start()
    pick_copy = pltpu.make_async_copy(pick_v, pick, in_sem.at[5])
    my_lane = lax.rem(me, groups_in_tile) * frows
    loads[0].wait()

    def swapped(value):
        return pltpu.roll(value, width, axis=1)

    for b in range(srows // 8):
        for l in range(sub):
            low, high = src[l, 8 * b:8 * b + 8, :], src[sub + l, 8 * b:8 * b + 8, :]
            place = pl.ds(8 * b, 8)
            own[0][place, l, :] = jnp.where(lane_8 < width, low, swapped(high))
            own[1][place, l, :] = jnp.where(lane_8 < width, swapped(low), high)

    table_copy.wait()
    pl.semaphore_wait(barrier, total)

    def chain_copy(h, up, t):
        boxes = (ups if up else downs)[h]
        return pltpu.make_async_remote_copy(
            src_ref=own[h] if t == 0 else boxes[t - 1], dst_ref=boxes[t],
            send_sem=chain_send.at[h, 0 if up else 1, t], recv_sem=chain_recv.at[h, 0 if up else 1, t],
            device_id=(x, y + (inner if up else -inner), lev), device_id_type=MESH)

    def slot_copy(h, q, tile):
        c = lax.rem(column + q, columns)
        sem = (h * columns + q) * depth + tile
        return pltpu.make_async_remote_copy(
            src_ref=outbox.at[h, pl.ds((c * depth + tile) * capacity, capacity)],
            dst_ref=inboxes[h].at[pl.ds((column * depth + tile) * capacity, capacity)],
            send_sem=send_sem.at[sem], recv_sem=recv_sem.at[sem],
            device_id=column_id(c), device_id_type=MESH)

    def ship(h, chunk, tile):
        def fill(c, write):
            owner = c // inner * along_y + z * inner + lax.rem(c, inner)
            for j in range(capacity):
                write((c * depth + tile) * capacity + j, chunk[table[owner, tile * capacity + j]])

        def to_outbox(n, value):
            outbox[h, n] = value

        def to_inbox(n, value):
            inboxes[h][n] = value

        def peer(q, carry):
            fill(lax.rem(column + q, columns), to_outbox)
            slot_copy(h, q, tile).start()
            return carry

        lax.fori_loop(1, columns, peer, 0)
        fill(column, to_inbox)

    def start_chain(h):
        if depth > 1:
            @pl.when(z < depth - 1)
            def _():
                chain_copy(h, True, 0).start()

            @pl.when(z > 0)
            def _():
                chain_copy(h, False, 0).start()

    def pass_on(h, t):
        for up, ok, onward in ((True, z >= t + 1, z < depth - 1), (False, z + 1 + t <= depth - 1, z > 0)):
            @pl.when(ok)
            def _():
                chain_copy(h, up, t).wait_recv()
                if t + 1 < depth - 1:
                    @pl.when(onward)
                    def _():
                        chain_copy(h, up, t + 1).start()
                ship(h, (ups if up else downs)[h][t], z - 1 - t if up else z + 1 + t)

    def s_copy(k):
        ok, device = near(*DIRS[k])
        return ok, pltpu.make_async_remote_copy(
            src_ref=smooth, dst_ref=s_in.at[OPPOSITE[k]], send_sem=s_send.at[k],
            recv_sem=s_recv.at[OPPOSITE[k]], device_id=device, device_id_type=MESH)

    def h_copy(k, tile):
        dx, dy = DIRS[k]
        ok, device = near(dx, dy)
        if dy == 0:
            source = main_a.at[pl.ds(frows if dx > 0 else PASSES, PASSES)]
            target = main_a.at[pl.ds(0 if dx > 0 else frows + PASSES, PASSES)]
        else:
            source, target = edge.at[tile], edge_in.at[OPPOSITE[k], tile]
        return ok, pltpu.make_async_remote_copy(
            src_ref=source, dst_ref=target, send_sem=h_send.at[k, tile],
            recv_sem=h_recv.at[OPPOSITE[k], tile], device_id=device, device_id_type=MESH)

    def split_weights(n):
        w_copy(n).wait()

        def one(i, carry):
            for k in range(fan):
                for h in range(HALVES):
                    value = w_full[i, pl.ds(k * LANES + h * width, width), :]
                    high = value.astype(jnp.bfloat16)
                    place = pl.ds(k * width, width)
                    w_high[h, i, place, :] = high
                    w_low[h, i, place, :] = (value - high.astype(jnp.float32)).astype(jnp.bfloat16)
            return carry

        lax.fori_loop(n * share, (n + 1) * share, one, 0)

    def product(h, i):
        rows = [[], []]
        for k in range(0, fan, 2):
            even, odd = (inboxes[h][pick[k + j, my_lane + i]] for j in range(2))
            rows[0].append(jnp.where(lane_8 < width, even, swapped(odd)))
            rows[1].append(jnp.where(lane_8 < width, swapped(even), odd))
        blocks = jnp.concatenate([jnp.concatenate(r, axis=1) for r in rows], axis=0)
        high = blocks.astype(jnp.bfloat16)
        low = (blocks - high.astype(jnp.float32)).astype(jnp.bfloat16)
        both = jnp.dot(jnp.concatenate([high, low], axis=0), w_high[h, i], preferred_element_type=jnp.float32)
        rest = jnp.dot(high, w_low[h, i], preferred_element_type=jnp.float32)
        result = both[:levels] + (both[levels:] + rest)
        if h == 0:
            main_a[PASSES + i] = result
        else:
            main_a[PASSES + i] += result

    groups = frows // GROUP

    def products(h, start, stop):
        def some(n, carry):
            for j in range(GROUP):
                product(h, n * GROUP + j)
            return carry

        lax.fori_loop(start, stop, some, 0)

    def landed(h):
        def one(n, carry):
            slot_copy(h, n // depth, lax.rem(n, depth)).wait_recv()
            return carry

        lax.fori_loop(depth, columns * depth, one, 0)

    start_chain(0)
    ship(0, own[0], z)
    ship(1, own[1], z)
    for k in range(len(DIRS)):
        ok, copy = s_copy(k)

        @pl.when(ok)
        def _():
            copy.start()

    for k, (dx, dy) in enumerate(DIRS):
        ok, _ = near(dx, dy)

        @pl.when(jnp.logical_not(ok))
        def _():
            s_in[k] = jnp.zeros(s_in.shape[1:], jnp.float32)
            if dy == 0:
                main_a[pl.ds(0 if dx < 0 else frows + PASSES, PASSES)] = jnp.zeros(
                    (PASSES,) + main_a.shape[1:], jnp.float32)
            else:
                edge_in[k] = jnp.zeros(edge_in.shape[1:], jnp.float32)

    span = pl.ds(pl.multiple_of(me // groups_in_tile * LANES, LANES), LANES)
    every = lax.broadcasted_iota(jnp.int32, (along_x * along_y, LANES), 0)
    named = [devices[k:k + 1, span] for k in range(fan)]
    hits = [jnp.where(named[k] == every, 1.0, 0.0) for k in range(fan)]
    found = ranks(hits)
    for k in range(fan):
        rank = jnp.sum(hits[k] * found[k], axis=0, keepdims=True).astype(jnp.int32)
        tile_y = lax.rem(named[k], along_y)
        base = (named[k] // along_y * inner + lax.rem(tile_y, inner)) * depth + tile_y // inner
        pick_v[k:k + 1, :] = jnp.clip(base * capacity + rank, 0, columns * depth * capacity - 1)
    pick_copy.start()

    done = 0
    events = sorted((t + 1.5 * h, h, t) for h in range(HALVES) for t in range(depth - 1))
    for n, (_, h, t) in enumerate(events):
        pass_on(h, t)
        if n == 0:
            start_chain(1)
        if done < W_PIECES:
            split_weights(done)
            done += 1
    for n in range(done, W_PIECES):
        split_weights(n)

    for k in range(len(DIRS)):
        ok, copy = s_copy(k)

        @pl.when(ok)
        def _():
            copy.wait_send()
            arrival_wait(s_in.at[k], smooth, s_recv.at[k])

    row_lane = lax.broadcasted_iota(jnp.int32, (1, LANES), 1)

    def side(left, right):
        return jnp.where(row_lane < PASSES, right, jnp.where(row_lane >= LANES - PASSES, left, 0.0))

    for i in range(frows):
        s_main[PASSES + i] = smooth[i:i + 1, :]
        s_side[PASSES + i] = side(s_in[at[0, -1], i:i + 1, :], s_in[at[0, 1], i:i + 1, :])
    for i in range(PASSES):
        low, high = frows - PASSES + i, frows + PASSES + i
        s_main[i] = s_in[at[-1, 0], low:low + 1, :]
        s_side[i] = side(s_in[at[-1, -1], low:low + 1, :], s_in[at[-1, 1], low:low + 1, :])
        s_main[high] = s_in[at[1, 0], i:i + 1, :]
        s_side[high] = side(s_in[at[1, -1], i:i + 1, :], s_in[at[1, 1], i:i + 1, :])

    landed(0)
    pick_copy.wait()
    products(0, 0, groups)
    landed(1)

    def send_halo(wanted):
        for k, (dx, dy) in enumerate(DIRS):
            for tile in wanted(dx, dy):
                ok, copy = h_copy(k, tile)

                @pl.when(ok)
                def _():
                    copy.start()

    def halo_tiles(dx, dy):
        if dy == 0:
            return [0]
        return list(range(tiles)) if dx == 0 else [0 if dx < 0 else tiles - 1]

    def pack(b):
        packed = jnp.zeros((levels, LANES), jnp.float32)
        for j in range(PER_TILE):
            moved = pltpu.roll(main_a[PASSES + b * PER_TILE + j], STRIP * j + STRIP // 2, axis=1)
            packed = jnp.where(lane // STRIP == j, moved, packed)
        edge[b] = packed
        send_halo(lambda dx, dy: [b] if dy != 0 and b in halo_tiles(dx, dy) else [])

    products(1, 0, 1)
    products(1, groups - 1, groups)
    send_halo(lambda dx, dy: [0] if dy == 0 else [])
    for b in range(tiles):
        products(1, max(1, b * groups // tiles), min(groups - 1, (b + 1) * groups // tiles))
        pack(b)

    def sent(n, carry):
        for h in range(HALVES):
            slot_copy(h, n // depth, lax.rem(n, depth)).wait_send()
        return carry

    lax.fori_loop(depth, columns * depth, sent, 0)
    for t in range(depth - 1):
        for h in range(HALVES):
            @pl.when(jnp.logical_and(z < depth - 1, z - t >= 0))
            def _():
                chain_copy(h, True, t).wait_send()

            @pl.when(jnp.logical_and(z > 0, z + t <= depth - 1))
            def _():
                chain_copy(h, False, t).wait_send()

    for k, (dx, dy) in enumerate(DIRS):
        for tile in halo_tiles(dx, dy):
            ok, copy = h_copy(k, tile)

            @pl.when(ok)
            def _():
                copy.wait_send()

        for tile in halo_tiles(-dx, -dy):
            @pl.when(near(dx, dy)[0])
            def _():
                if dy == 0:
                    rows = main_a.at[pl.ds(0 if dx < 0 else frows + PASSES, PASSES)]
                    arrival_wait(rows, rows, h_recv.at[k, tile])
                else:
                    arrival_wait(edge_in.at[k, tile], edge.at[tile], h_recv.at[k, tile])

    inside = jnp.logical_or(lane < PASSES, lane >= LANES - PASSES)

    def unpack(row, tile, place, left, right):
        merged = jnp.where(lax.rem(lane, STRIP) < STRIP // 2, edge_in[left, tile], edge_in[right, tile])
        moved = pltpu.roll(merged, (2 * LANES - STRIP * place - STRIP // 2) % LANES, axis=1)
        side_a[row] = jnp.where(inside, moved, 0.0)

    for i in range(frows):
        unpack(PASSES + i, i // PER_TILE, i % PER_TILE, at[0, -1], at[0, 1])
    for i in range(PASSES):
        far = frows - PASSES + i
        unpack(i, far // PER_TILE, far % PER_TILE, at[-1, -1], at[-1, 1])
        unpack(frows + PASSES + i, 0, i, at[1, -1], at[1, 1])

    first, last = lane == 0, lane == LANES - 1

    def smooth_row(r, main, sides, write):
        u, h = main[r], sides[r]
        u_up, u_down = pltpu.roll(u, 1, axis=1), pltpu.roll(u, LANES - 1, axis=1)
        h_up, h_down = pltpu.roll(h, 1, axis=1), pltpu.roll(h, LANES - 1, axis=1)
        lap = (main[r + 1] + main[r - 1] + jnp.where(last, h_down, u_down)
               + jnp.where(first, h_up, u_up) - 4.0 * u)
        lap_h = (sides[r + 1] + sides[r - 1] + jnp.where(last, u_down, h_down)
                 + jnp.where(first, u_up, h_up) - 4.0 * h)
        write(r, u, s_main[r] * lap, h + s_side[r] * lap_h)

    def write_b(r, u, step, h):
        main_b[r] = u + step
        side_b[r] = h

    def write_a(r, u, step, h):
        main_a[r] = u + step
        side_a[r] = h

    def write_out(r, u, step, h):
        place = pl.ds(r - PASSES, levels, stride=frows)
        out[place, :] = u
        change[place, :] = step

    for p, (main, sides, write) in enumerate((
            (main_a, side_a, write_b), (main_b, side_b, write_a), (main_a, side_a, write_out))):
        start, count = p + 1, frows + 2 * PASSES - 2 * (p + 1)
        chunk = next(n for n in (12, 17, 16, 2, 1) if count % n == 0)

        def rows(n, carry):
            for j in range(chunk):
                smooth_row(start + n * chunk + j, main, sides, write)
            return carry

        lax.fori_loop(0, count // chunk, rows, 0)


def arrival_wait(target, source, sem):
    pltpu.make_async_copy(source, target, sem).wait()


def shards(source, remap_weights, intersection_devices, intersection_rows, smoothing):
    along_x = lax.axis_size("gx")
    along_y = lax.axis_size("gy")
    devices = along_x * along_y
    frows, fanin, block = remap_weights.shape[:3]
    levels, srows = source.shape[:2]
    capacity = 2 * max(1, frows * fanin // devices)
    depth, inner = layout(along_x, along_y, capacity, srows)
    columns = along_x * inner
    full = frows + 2 * PASSES
    sub = levels // HALVES
    vmem = functools.partial(pltpu.VMEM, dtype=jnp.float32)
    tile = (levels, block)
    in_vmem = pl.BlockSpec(memory_space=pltpu.VMEM)
    anywhere = pl.BlockSpec(memory_space=pl.ANY)
    entries = (fanin, intersection_devices.shape[0])
    tables = ((devices, -(-depth * capacity // block) * block), (fanin, block))
    slots_all = columns * depth * capacity
    dma = pltpu.SemaphoreType.DMA
    sides = len(DIRS)
    edges = frows // PER_TILE
    halves = pltpu.VMEM((HALVES, frows, fanin * block // HALVES, block), jnp.bfloat16)
    field, change = pl.pallas_call(
        functools.partial(kernel, (along_x, along_y, depth, inner, capacity)),
        out_shape=[jax.ShapeDtypeStruct((levels * frows, block), jnp.float32)] * 2,
        in_specs=[anywhere] * 5,
        out_specs=[in_vmem] * 2,
        scratch_shapes=[
            pltpu.VMEM(entries, jnp.int32), pltpu.VMEM(entries, jnp.int32),
            vmem((levels, srows, block)), vmem((frows, block)),
            *[pltpu.VMEM(shape, jnp.int32) for shape in tables],
            *[pltpu.SMEM(shape, jnp.int32) for shape in tables],
            vmem((slots_all, sub, block)), vmem((slots_all, sub, block)),
            vmem((HALVES, slots_all, sub, block)),
            vmem((frows, fanin * block, block)),
            halves, halves,
            vmem((full,) + tile), vmem((full,) + tile), vmem((full,) + tile), vmem((full,) + tile),
            vmem((full, 1, block)), vmem((full, 1, block)),
            vmem((sides, frows, block)),
            vmem((edges,) + tile),
            vmem((sides, edges) + tile),
            dma((HALVES * columns * depth,)), dma((HALVES * columns * depth,)),
            dma((HALVES, 2, max(1, depth - 1))), dma((HALVES, 2, max(1, depth - 1))),
            dma((sides,)), dma((sides,)), dma((sides, edges)), dma((sides, edges)),
            dma((W_PIECES,)), dma((6,)),
        ] + [vmem((srows, sub, block))] * (HALVES + 2 * HALVES * (depth - 1)),
        compiler_params=pltpu.CompilerParams(
            collective_id=0, has_side_effects=True, vmem_limit_bytes=56 * 2 ** 20),
        cost_estimate=pl.CostEstimate(
            flops=6 * levels * frows * fanin * block * block, bytes_accessed=16 * 2 ** 20, transcendentals=0),
    )(intersection_devices.T, intersection_rows.T, source, remap_weights.reshape(frows, fanin * block, block), smoothing)
    return (field + change).reshape(levels, frows, block)


def solution(mesh):
    return jax.shard_map(
        shards,
        mesh=mesh,
        in_specs=(P("lev", "gy", "gx"), P(("gx", "gy"), None, None, None), P(), P(), P("gx", "gy")),
        out_specs=P("lev", "gx", "gy"),
        check_vma=False,
    )
```

```python
import functools

import jax
import jax.numpy as jnp
from jax import lax
from jax.experimental import pallas as pl
from jax.experimental.pallas import tpu as pltpu
from jax.sharding import PartitionSpec as P

PASSES = 3
MESH = pl.DeviceIdType.MESH
DIRS = [(dx, dy) for dx in (-1, 0, 1) for dy in (-1, 0, 1) if (dx, dy) != (0, 0)]
OPPOSITE = [DIRS.index((-dx, -dy)) for dx, dy in DIRS]
LANES = 128
STRIP = 8
PER_TILE = LANES // STRIP
HALVES = 2
W_PIECES = 4
GROUP = 8


def layout(along_x, along_y, capacity, rows):
    inner = 2 if along_y % 2 == 0 else 1
    if capacity * inner * along_x > rows:
        return along_y // inner, inner
    return 1, along_y


def kernel(dims, devices_in, rows_in, src_in, weights, smooth_in, out, devices, lat, src, smooth,
           table_v, pick_v, table, pick, inbox_0, inbox_1, outbox, w_full, w_high, w_low,
           main_a, main_b, side_a, side_b, s_main, s_side, s_in, edge, edge_in,
           send_sem, recv_sem, chain_send, chain_recv, s_send, s_recv, h_send, h_recv, w_sem, in_sem, *chunks):
    along_x, along_y, depth, inner, capacity = dims
    frows, fan = w_full.shape[0], devices.shape[0]
    levels, srows = src.shape[:2]
    sub = levels // HALVES
    width = LANES // HALVES
    columns = along_x * inner
    inboxes = (inbox_0, inbox_1)
    own, chain = chunks[:HALVES], chunks[HALVES:]
    ups = [chain[h * (depth - 1):(h + 1) * (depth - 1)] for h in range(HALVES)]
    downs = [chain[(HALVES + h) * (depth - 1):(HALVES + h + 1) * (depth - 1)] for h in range(HALVES)]
    x, y, lev = lax.axis_index("gx"), lax.axis_index("gy"), lax.axis_index("lev")
    z, yi = y // inner, y % inner
    column = x * inner + yi
    lane = lax.broadcasted_iota(jnp.int32, (levels, LANES), 1)
    lane_8 = lax.broadcasted_iota(jnp.int32, (sub, LANES), 1)
    tiles = frows // PER_TILE
    at = {d: k for k, d in enumerate(DIRS)}

    def column_id(c):
        return (c // inner, z * inner + c % inner, lev)

    def near(dx, dy):
        ok = jnp.logical_and(
            jnp.logical_and(x + dx >= 0, x + dx < along_x),
            jnp.logical_and(y + dy >= 0, y + dy < along_y),
        )
        return ok, (x + dx, y + dy, lev)

    loads = [pltpu.make_async_copy(a, b, in_sem.at[n]) for n, (a, b) in enumerate((
        (src_in, src), (devices_in, devices), (rows_in, lat), (smooth_in, smooth)))]
    for load in loads:
        load.start()

    barrier = pltpu.get_barrier_semaphore()

    def greet(device):
        pl.semaphore_signal(barrier, inc=1, device_id=device, device_id_type=MESH)

    def greet_column(q, carry):
        greet(column_id(lax.rem(column + q, columns)))
        return carry

    lax.fori_loop(1, columns, greet_column, 0)
    total = columns - 1
    links = [near(dx, dy) for dx, dy in DIRS]
    if depth > 1:
        links = links + [(z < depth - 1, (x, y + inner, lev)), (z > 0, (x, y - inner, lev))]
    for ok, device in links:
        total = total + ok.astype(jnp.int32)

        @pl.when(ok)
        def _():
            greet(device)

    share = frows // W_PIECES

    def w_copy(n):
        rows = pl.ds(n * share, share)
        return pltpu.make_async_copy(weights.at[rows], w_full.at[rows], w_sem.at[n])

    for n in range(W_PIECES):
        w_copy(n).start()

    for load in loads[1:]:
        load.wait()
    me = x * along_y + y
    wide = (LANES, LANES)
    from_lane = lax.broadcasted_iota(jnp.int32, wide, 0)
    to_lane = lax.broadcasted_iota(jnp.int32, wide, 1)
    together = from_lane // frows == to_lane // frows
    group_ones = jnp.where(together, 1.0, 0.0).astype(jnp.bfloat16)
    earlier = jnp.where(jnp.logical_and(together, from_lane < to_lane), 1.0, 0.0).astype(jnp.bfloat16)

    def count(hits, matrix):
        return jnp.dot(hits.astype(jnp.bfloat16), matrix, preferred_element_type=jnp.float32)

    def ranks(hits):
        found, before = [], None
        for k in range(fan):
            within = count(hits[k], earlier)
            found.append(within if before is None else within + before)
            if k + 1 < fan:
                whole = count(hits[k], group_ones)
                before = whole if before is None else before + whole
        return found

    groups_in_tile = LANES // frows
    slot = lax.broadcasted_iota(jnp.int32, (capacity, LANES), 0).astype(jnp.float32)
    mine = lax.broadcasted_iota(jnp.int32, (max(8, depth), LANES), 0) * inner + x * along_y + yi
    rows_of = jnp.zeros(table_v.shape, jnp.float32)
    spare = table_v.shape[1] - depth * capacity
    for n in range(devices.shape[1] // LANES):
        span = slice(n * LANES, (n + 1) * LANES)
        hits = [jnp.where(devices[k:k + 1, span] == mine, 1.0, 0.0) for k in range(fan)]
        found = ranks(hits)
        parts = []
        for t in range(depth):
            part = jnp.zeros((capacity, LANES), jnp.float32)
            for k in range(fan):
                rank = jnp.where(hits[k][t:t + 1] > 0.5, found[k][t:t + 1], -1.0)
                part = part + jnp.where(rank == slot, lat[k:k + 1, span].astype(jnp.float32), 0.0)
            parts.append(part)
        if spare:
            parts.append(jnp.zeros((spare, LANES), jnp.float32))
        owner = lax.broadcasted_iota(jnp.int32, (table_v.shape[0], LANES), 0)
        lane_of = lax.broadcasted_iota(jnp.int32, (table_v.shape[0], LANES), 1)
        gather = jnp.where(lane_of // frows + n * groups_in_tile == owner, 1.0, 0.0).astype(jnp.bfloat16)
        rows_of = rows_of + lax.dot_general(
            gather, jnp.concatenate(parts, axis=0).astype(jnp.bfloat16), (((1,), (1,)), ((), ())),
            preferred_element_type=jnp.float32)
    table_v[...] = jnp.clip(rows_of.astype(jnp.int32), 0, srows - 1)

    table_copy = pltpu.make_async_copy(table_v, table, in_sem.at[4])
    table_copy.start()
    pick_copy = pltpu.make_async_copy(pick_v, pick, in_sem.at[5])
    my_lane = lax.rem(me, groups_in_tile) * frows
    loads[0].wait()

    def swapped(value):
        return pltpu.roll(value, width, axis=1)

    for b in range(srows // 8):
        for l in range(sub):
            low, high = src[l, 8 * b:8 * b + 8, :], src[sub + l, 8 * b:8 * b + 8, :]
            place = pl.ds(8 * b, 8)
            own[0][place, l, :] = jnp.where(lane_8 < width, low, swapped(high))
            own[1][place, l, :] = jnp.where(lane_8 < width, swapped(low), high)

    table_copy.wait()
    pl.semaphore_wait(barrier, total)

    def chain_copy(h, up, t):
        boxes = (ups if up else downs)[h]
        return pltpu.make_async_remote_copy(
            src_ref=own[h] if t == 0 else boxes[t - 1], dst_ref=boxes[t],
            send_sem=chain_send.at[h, 0 if up else 1, t], recv_sem=chain_recv.at[h, 0 if up else 1, t],
            device_id=(x, y + (inner if up else -inner), lev), device_id_type=MESH)

    def slot_copy(h, q, tile):
        c = lax.rem(column + q, columns)
        sem = (h * columns + q) * depth + tile
        return pltpu.make_async_remote_copy(
            src_ref=outbox.at[h, pl.ds((c * depth + tile) * capacity, capacity)],
            dst_ref=inboxes[h].at[pl.ds((column * depth + tile) * capacity, capacity)],
            send_sem=send_sem.at[sem], recv_sem=recv_sem.at[sem],
            device_id=column_id(c), device_id_type=MESH)

    def ship(h, chunk, tile):
        def fill(c, write):
            owner = c // inner * along_y + z * inner + lax.rem(c, inner)
            for j in range(capacity):
                write((c * depth + tile) * capacity + j, chunk[table[owner, tile * capacity + j]])

        def to_outbox(n, value):
            outbox[h, n] = value

        def to_inbox(n, value):
            inboxes[h][n] = value

        def peer(n, carry):
            q = jnp.where(lev % 2 == 0, n, columns - n)
            fill(lax.rem(column + q, columns), to_outbox)
            slot_copy(h, q, tile).start()
            return carry

        lax.fori_loop(1, columns, peer, 0)
        fill(column, to_inbox)

    def start_chain(h):
        if depth > 1:
            @pl.when(z < depth - 1)
            def _():
                chain_copy(h, True, 0).start()

            @pl.when(z > 0)
            def _():
                chain_copy(h, False, 0).start()

    def pass_on(h, t):
        for up, ok, onward in ((True, z >= t + 1, z < depth - 1), (False, z + 1 + t <= depth - 1, z > 0)):
            @pl.when(ok)
            def _():
                chain_copy(h, up, t).wait_recv()
                if t + 1 < depth - 1:
                    @pl.when(onward)
                    def _():
                        chain_copy(h, up, t + 1).start()
                ship(h, (ups if up else downs)[h][t], z - 1 - t if up else z + 1 + t)

    def s_copy(k):
        ok, device = near(*DIRS[k])
        return ok, pltpu.make_async_remote_copy(
            src_ref=smooth, dst_ref=s_in.at[OPPOSITE[k]], send_sem=s_send.at[k],
            recv_sem=s_recv.at[OPPOSITE[k]], device_id=device, device_id_type=MESH)

    def h_copy(k, tile):
        dx, dy = DIRS[k]
        ok, device = near(dx, dy)
        if dy == 0:
            source = main_a.at[pl.ds(frows if dx > 0 else PASSES, PASSES)]
            target = main_a.at[pl.ds(0 if dx > 0 else frows + PASSES, PASSES)]
        else:
            source, target = edge.at[tile], edge_in.at[OPPOSITE[k], tile]
        return ok, pltpu.make_async_remote_copy(
            src_ref=source, dst_ref=target, send_sem=h_send.at[k, tile],
            recv_sem=h_recv.at[OPPOSITE[k], tile], device_id=device, device_id_type=MESH)

    def split_weights(n):
        w_copy(n).wait()

        def one(i, carry):
            for k in range(fan):
                for h in range(HALVES):
                    value = w_full[i, pl.ds(k * LANES + h * width, width), :]
                    high = value.astype(jnp.bfloat16)
                    place = pl.ds(k * width, width)
                    w_high[h, i, place, :] = high
                    w_low[h, i, place, :] = (value - high.astype(jnp.float32)).astype(jnp.bfloat16)
            return carry

        lax.fori_loop(n * share, (n + 1) * share, one, 0)

    def product(h, i):
        rows = [[], []]
        for k in range(0, fan, 2):
            even, odd = (inboxes[h][pick[k + j, my_lane + i]] for j in range(2))
            rows[0].append(jnp.where(lane_8 < width, even, swapped(odd)))
            rows[1].append(jnp.where(lane_8 < width, swapped(even), odd))
        blocks = jnp.concatenate([jnp.concatenate(r, axis=1) for r in rows], axis=0)
        high = blocks.astype(jnp.bfloat16)
        low = (blocks - high.astype(jnp.float32)).astype(jnp.bfloat16)
        both = jnp.dot(jnp.concatenate([high, low], axis=0), w_high[h, i], preferred_element_type=jnp.float32)
        rest = jnp.dot(high, w_low[h, i], preferred_element_type=jnp.float32)
        result = both[:levels] + (both[levels:] + rest)
        if h == 0:
            main_a[PASSES + i] = result
        else:
            main_a[PASSES + i] += result

    groups = frows // GROUP

    def products(h, start, stop):
        def some(n, carry):
            for j in range(GROUP):
                product(h, n * GROUP + j)
            return carry

        lax.fori_loop(start, stop, some, 0)

    def landed(h):
        def one(n, carry):
            slot_copy(h, n // depth, lax.rem(n, depth)).wait_recv()
            return carry

        lax.fori_loop(depth, columns * depth, one, 0)

    start_chain(0)
    ship(0, own[0], z)
    ship(1, own[1], z)
    for k in range(len(DIRS)):
        ok, copy = s_copy(k)

        @pl.when(ok)
        def _():
            copy.start()

    for k, (dx, dy) in enumerate(DIRS):
        ok, _ = near(dx, dy)

        @pl.when(jnp.logical_not(ok))
        def _():
            s_in[k] = jnp.zeros(s_in.shape[1:], jnp.float32)
            if dy == 0:
                main_a[pl.ds(0 if dx < 0 else frows + PASSES, PASSES)] = jnp.zeros(
                    (PASSES,) + main_a.shape[1:], jnp.float32)
            else:
                edge_in[k] = jnp.zeros(edge_in.shape[1:], jnp.float32)

    span = pl.ds(pl.multiple_of(me // groups_in_tile * LANES, LANES), LANES)
    every = lax.broadcasted_iota(jnp.int32, (along_x * along_y, LANES), 0)
    named = [devices[k:k + 1, span] for k in range(fan)]
    hits = [jnp.where(named[k] == every, 1.0, 0.0) for k in range(fan)]
    found = ranks(hits)
    for k in range(fan):
        rank = jnp.sum(hits[k] * found[k], axis=0, keepdims=True).astype(jnp.int32)
        tile_y = lax.rem(named[k], along_y)
        base = (named[k] // along_y * inner + lax.rem(tile_y, inner)) * depth + tile_y // inner
        pick_v[k:k + 1, :] = jnp.clip(base * capacity + rank, 0, columns * depth * capacity - 1)
    pick_copy.start()

    done = 0
    events = sorted((t + 1.5 * h, h, t) for h in range(HALVES) for t in range(depth - 1))
    for n, (_, h, t) in enumerate(events):
        pass_on(h, t)
        if n == 0:
            start_chain(1)
        if done < W_PIECES:
            split_weights(done)
            done += 1
    for n in range(done, W_PIECES):
        split_weights(n)

    for k in range(len(DIRS)):
        ok, copy = s_copy(k)

        @pl.when(ok)
        def _():
            copy.wait_send()
            arrival_wait(s_in.at[k], smooth, s_recv.at[k])

    row_lane = lax.broadcasted_iota(jnp.int32, (1, LANES), 1)

    def side(left, right):
        return jnp.where(row_lane < PASSES, right, jnp.where(row_lane >= LANES - PASSES, left, 0.0))

    for i in range(frows):
        s_main[PASSES + i] = smooth[i:i + 1, :]
        s_side[PASSES + i] = side(s_in[at[0, -1], i:i + 1, :], s_in[at[0, 1], i:i + 1, :])
    for i in range(PASSES):
        low, high = frows - PASSES + i, frows + PASSES + i
        s_main[i] = s_in[at[-1, 0], low:low + 1, :]
        s_side[i] = side(s_in[at[-1, -1], low:low + 1, :], s_in[at[-1, 1], low:low + 1, :])
        s_main[high] = s_in[at[1, 0], i:i + 1, :]
        s_side[high] = side(s_in[at[1, -1], i:i + 1, :], s_in[at[1, 1], i:i + 1, :])

    landed(0)
    pick_copy.wait()
    products(0, 0, groups)
    landed(1)

    def send_halo(wanted):
        for k, (dx, dy) in enumerate(DIRS):
            for tile in wanted(dx, dy):
                ok, copy = h_copy(k, tile)

                @pl.when(ok)
                def _():
                    copy.start()

    def halo_tiles(dx, dy):
        if dy == 0:
            return [0]
        return list(range(tiles)) if dx == 0 else [0 if dx < 0 else tiles - 1]

    def pack(b):
        packed = jnp.zeros((levels, LANES), jnp.float32)
        for j in range(PER_TILE):
            moved = pltpu.roll(main_a[PASSES + b * PER_TILE + j], STRIP * j + STRIP // 2, axis=1)
            packed = jnp.where(lane // STRIP == j, moved, packed)
        edge[b] = packed
        send_halo(lambda dx, dy: [b] if dy != 0 and b in halo_tiles(dx, dy) else [])

    products(1, 0, 1)
    products(1, groups - 1, groups)
    send_halo(lambda dx, dy: [0] if dy == 0 else [])
    for b in range(tiles):
        products(1, max(1, b * groups // tiles), min(groups - 1, (b + 1) * groups // tiles))
        pack(b)

    def sent(n, carry):
        for h in range(HALVES):
            slot_copy(h, n // depth, lax.rem(n, depth)).wait_send()
        return carry

    lax.fori_loop(depth, columns * depth, sent, 0)
    for t in range(depth - 1):
        for h in range(HALVES):
            @pl.when(jnp.logical_and(z < depth - 1, z - t >= 0))
            def _():
                chain_copy(h, True, t).wait_send()

            @pl.when(jnp.logical_and(z > 0, z + t <= depth - 1))
            def _():
                chain_copy(h, False, t).wait_send()

    for k, (dx, dy) in enumerate(DIRS):
        for tile in halo_tiles(dx, dy):
            ok, copy = h_copy(k, tile)

            @pl.when(ok)
            def _():
                copy.wait_send()

        for tile in halo_tiles(-dx, -dy):
            @pl.when(near(dx, dy)[0])
            def _():
                if dy == 0:
                    rows = main_a.at[pl.ds(0 if dx < 0 else frows + PASSES, PASSES)]
                    arrival_wait(rows, rows, h_recv.at[k, tile])
                else:
                    arrival_wait(edge_in.at[k, tile], edge.at[tile], h_recv.at[k, tile])

    inside = jnp.logical_or(lane < PASSES, lane >= LANES - PASSES)

    def unpack(row, tile, place, left, right):
        merged = jnp.where(lax.rem(lane, STRIP) < STRIP // 2, edge_in[left, tile], edge_in[right, tile])
        moved = pltpu.roll(merged, (2 * LANES - STRIP * place - STRIP // 2) % LANES, axis=1)
        side_a[row] = jnp.where(inside, moved, 0.0)

    for i in range(frows):
        unpack(PASSES + i, i // PER_TILE, i % PER_TILE, at[0, -1], at[0, 1])
    for i in range(PASSES):
        far = frows - PASSES + i
        unpack(i, far // PER_TILE, far % PER_TILE, at[-1, -1], at[-1, 1])
        unpack(frows + PASSES + i, 0, i, at[1, -1], at[1, 1])

    first, last = lane == 0, lane == LANES - 1

    def smooth_row(r, main, sides, write):
        u, h = main[r], sides[r]
        u_up, u_down = pltpu.roll(u, 1, axis=1), pltpu.roll(u, LANES - 1, axis=1)
        h_up, h_down = pltpu.roll(h, 1, axis=1), pltpu.roll(h, LANES - 1, axis=1)
        lap = (main[r + 1] + main[r - 1] + jnp.where(last, h_down, u_down)
               + jnp.where(first, h_up, u_up) - 4.0 * u)
        lap_h = (sides[r + 1] + sides[r - 1] + jnp.where(last, u_down, h_down)
                 + jnp.where(first, u_up, h_up) - 4.0 * h)
        write(r, u, s_main[r] * lap, h + s_side[r] * lap_h)

    def write_b(r, u, step, h):
        main_b[r] = u + step
        side_b[r] = h

    def write_a(r, u, step, h):
        main_a[r] = u + step
        side_a[r] = h

    def write_out(r, u, step, h):
        out[pl.ds(r - PASSES, levels, stride=frows), :] = u + step

    for p, (main, sides, write) in enumerate((
            (main_a, side_a, write_b), (main_b, side_b, write_a), (main_a, side_a, write_out))):
        start, count = p + 1, frows + 2 * PASSES - 2 * (p + 1)
        chunk = next(n for n in (12, 17, 16, 2, 1) if count % n == 0)

        def rows(n, carry):
            for j in range(chunk):
                smooth_row(start + n * chunk + j, main, sides, write)
            return carry

        lax.fori_loop(0, count // chunk, rows, 0)


def arrival_wait(target, source, sem):
    pltpu.make_async_copy(source, target, sem).wait()


def shards(source, remap_weights, intersection_devices, intersection_rows, smoothing):
    along_x = lax.axis_size("gx")
    along_y = lax.axis_size("gy")
    devices = along_x * along_y
    frows, fanin, block = remap_weights.shape[:3]
    levels, srows = source.shape[:2]
    capacity = 2 * max(1, frows * fanin // devices)
    depth, inner = layout(along_x, along_y, capacity, srows)
    columns = along_x * inner
    full = frows + 2 * PASSES
    sub = levels // HALVES
    vmem = functools.partial(pltpu.VMEM, dtype=jnp.float32)
    tile = (levels, block)
    in_vmem = pl.BlockSpec(memory_space=pltpu.VMEM)
    anywhere = pl.BlockSpec(memory_space=pl.ANY)
    entries = (fanin, intersection_devices.shape[0])
    tables = ((devices, -(-depth * capacity // block) * block), (fanin, block))
    slots_all = columns * depth * capacity
    dma = pltpu.SemaphoreType.DMA
    sides = len(DIRS)
    edges = frows // PER_TILE
    halves = pltpu.VMEM((HALVES, frows, fanin * block // HALVES, block), jnp.bfloat16)
    field = pl.pallas_call(
        functools.partial(kernel, (along_x, along_y, depth, inner, capacity)),
        out_shape=jax.ShapeDtypeStruct((levels * frows, block), jnp.float32),
        in_specs=[anywhere] * 5,
        out_specs=in_vmem,
        scratch_shapes=[
            pltpu.VMEM(entries, jnp.int32), pltpu.VMEM(entries, jnp.int32),
            vmem((levels, srows, block)), vmem((frows, block)),
            *[pltpu.VMEM(shape, jnp.int32) for shape in tables],
            *[pltpu.SMEM(shape, jnp.int32) for shape in tables],
            vmem((slots_all, sub, block)), vmem((slots_all, sub, block)),
            vmem((HALVES, slots_all, sub, block)),
            vmem((frows, fanin * block, block)),
            halves, halves,
            vmem((full,) + tile), vmem((full,) + tile), vmem((full,) + tile), vmem((full,) + tile),
            vmem((full, 1, block)), vmem((full, 1, block)),
            vmem((sides, frows, block)),
            vmem((edges,) + tile),
            vmem((sides, edges) + tile),
            dma((HALVES * columns * depth,)), dma((HALVES * columns * depth,)),
            dma((HALVES, 2, max(1, depth - 1))), dma((HALVES, 2, max(1, depth - 1))),
            dma((sides,)), dma((sides,)), dma((sides, edges)), dma((sides, edges)),
            dma((W_PIECES,)), dma((6,)),
        ] + [vmem((srows, sub, block))] * (HALVES + 2 * HALVES * (depth - 1)),
        compiler_params=pltpu.CompilerParams(
            collective_id=0, has_side_effects=True, vmem_limit_bytes=56 * 2 ** 20),
        cost_estimate=pl.CostEstimate(
            flops=6 * levels * frows * fanin * block * block, bytes_accessed=16 * 2 ** 20, transcendentals=0),
    )(intersection_devices.T, intersection_rows.T, source, remap_weights.reshape(frows, fanin * block, block), smoothing)
    return field.reshape(levels, frows, block)


def solution(mesh):
    return jax.shard_map(
        shards,
        mesh=mesh,
        in_specs=(P("lev", "gy", "gx"), P(("gx", "gy"), None, None, None), P(), P(), P("gx", "gy")),
        out_specs=P("lev", "gx", "gy"),
        check_vma=False,
    )
```

```python
import functools

import jax
import jax.numpy as jnp
from jax import lax
from jax.experimental import pallas as pl
from jax.experimental.pallas import tpu as pltpu
from jax.sharding import PartitionSpec as P

PASSES = 3
MESH = pl.DeviceIdType.MESH
DIRS = [(dx, dy) for dx in (-1, 0, 1) for dy in (-1, 0, 1) if (dx, dy) != (0, 0)]
OPPOSITE = [DIRS.index((-dx, -dy)) for dx, dy in DIRS]
LANES = 128
STRIP = 8
PER_TILE = LANES // STRIP
HALVES = 2
W_PIECES = 4
GROUP = 8


def layout(along_x, along_y, capacity, rows):
    inner = 2 if along_y % 2 == 0 else 1
    if capacity * inner * along_x > rows:
        return along_y // inner, inner
    return 1, along_y


def kernel(dims, devices_in, rows_in, src_in, weights, smooth_in, out, devices, lat, src, smooth,
           table_v, pick_v, table, pick, inbox_0, inbox_1, outbox, w_full, w_high, w_low,
           main_a, main_b, side_a, side_b, s_main, s_side, s_in, edge, edge_in,
           send_sem, recv_sem, chain_send, chain_recv, s_send, s_recv, h_send, h_recv, w_sem, in_sem, *chunks):
    along_x, along_y, depth, inner, capacity = dims
    frows, fan = w_full.shape[0], devices.shape[0]
    levels, srows = src.shape[:2]
    sub = levels // HALVES
    width = LANES // HALVES
    columns = along_x * inner
    inboxes = (inbox_0, inbox_1)
    own, chain = chunks[:HALVES], chunks[HALVES:]
    ups = [chain[h * (depth - 1):(h + 1) * (depth - 1)] for h in range(HALVES)]
    downs = [chain[(HALVES + h) * (depth - 1):(HALVES + h + 1) * (depth - 1)] for h in range(HALVES)]
    x, y, lev = lax.axis_index("gx"), lax.axis_index("gy"), lax.axis_index("lev")
    z, yi = y // inner, y % inner
    column = x * inner + yi
    lane = lax.broadcasted_iota(jnp.int32, (levels, LANES), 1)
    lane_8 = lax.broadcasted_iota(jnp.int32, (sub, LANES), 1)
    tiles = frows // PER_TILE
    at = {d: k for k, d in enumerate(DIRS)}

    def column_id(c):
        return (c // inner, z * inner + c % inner, lev)

    def near(dx, dy):
        ok = jnp.logical_and(
            jnp.logical_and(x + dx >= 0, x + dx < along_x),
            jnp.logical_and(y + dy >= 0, y + dy < along_y),
        )
        return ok, (x + dx, y + dy, lev)

    loads = [pltpu.make_async_copy(a, b, in_sem.at[n]) for n, (a, b) in enumerate((
        (src_in, src), (devices_in, devices), (rows_in, lat), (smooth_in, smooth)))]
    for load in loads:
        load.start()

    barrier = pltpu.get_barrier_semaphore()

    def greet(device):
        pl.semaphore_signal(barrier, inc=1, device_id=device, device_id_type=MESH)

    def greet_column(q, carry):
        greet(column_id(lax.rem(column + q, columns)))
        return carry

    lax.fori_loop(1, columns, greet_column, 0)
    total = columns - 1
    links = [near(dx, dy) for dx, dy in DIRS]
    if depth > 1:
        links = links + [(z < depth - 1, (x, y + inner, lev)), (z > 0, (x, y - inner, lev))]
    for ok, device in links:
        total = total + ok.astype(jnp.int32)

        @pl.when(ok)
        def _():
            greet(device)

    share = frows // W_PIECES

    def w_copy(n):
        rows = pl.ds(n * share, share)
        return pltpu.make_async_copy(weights.at[rows], w_full.at[rows], w_sem.at[n])

    for n in range(W_PIECES):
        w_copy(n).start()

    for load in loads[1:]:
        load.wait()
    me = x * along_y + y
    wide = (LANES, LANES)
    from_lane = lax.broadcasted_iota(jnp.int32, wide, 0)
    to_lane = lax.broadcasted_iota(jnp.int32, wide, 1)
    together = from_lane // frows == to_lane // frows
    group_ones = jnp.where(together, 1.0, 0.0).astype(jnp.bfloat16)
    earlier = jnp.where(jnp.logical_and(together, from_lane < to_lane), 1.0, 0.0).astype(jnp.bfloat16)

    def count(hits, matrix):
        return jnp.dot(hits.astype(jnp.bfloat16), matrix, preferred_element_type=jnp.float32)

    def ranks(hits):
        found, before = [], None
        for k in range(fan):
            within = count(hits[k], earlier)
            found.append(within if before is None else within + before)
            if k + 1 < fan:
                whole = count(hits[k], group_ones)
                before = whole if before is None else before + whole
        return found

    groups_in_tile = LANES // frows
    slot = lax.broadcasted_iota(jnp.int32, (capacity, LANES), 0).astype(jnp.float32)
    mine = lax.broadcasted_iota(jnp.int32, (max(8, depth), LANES), 0) * inner + x * along_y + yi
    rows_of = jnp.zeros(table_v.shape, jnp.float32)
    spare = table_v.shape[1] - depth * capacity
    for n in range(devices.shape[1] // LANES):
        span = slice(n * LANES, (n + 1) * LANES)
        hits = [jnp.where(devices[k:k + 1, span] == mine, 1.0, 0.0) for k in range(fan)]
        found = ranks(hits)
        parts = []
        for t in range(depth):
            part = jnp.zeros((capacity, LANES), jnp.float32)
            for k in range(fan):
                rank = jnp.where(hits[k][t:t + 1] > 0.5, found[k][t:t + 1], -1.0)
                part = part + jnp.where(rank == slot, lat[k:k + 1, span].astype(jnp.float32), 0.0)
            parts.append(part)
        if spare:
            parts.append(jnp.zeros((spare, LANES), jnp.float32))
        owner = lax.broadcasted_iota(jnp.int32, (table_v.shape[0], LANES), 0)
        lane_of = lax.broadcasted_iota(jnp.int32, (table_v.shape[0], LANES), 1)
        gather = jnp.where(lane_of // frows + n * groups_in_tile == owner, 1.0, 0.0).astype(jnp.bfloat16)
        rows_of = rows_of + lax.dot_general(
            gather, jnp.concatenate(parts, axis=0).astype(jnp.bfloat16), (((1,), (1,)), ((), ())),
            preferred_element_type=jnp.float32)
    table_v[...] = jnp.clip(rows_of.astype(jnp.int32), 0, srows - 1)

    table_copy = pltpu.make_async_copy(table_v, table, in_sem.at[4])
    table_copy.start()
    pick_copy = pltpu.make_async_copy(pick_v, pick, in_sem.at[5])
    my_lane = lax.rem(me, groups_in_tile) * frows
    loads[0].wait()

    def swapped(value):
        return pltpu.roll(value, width, axis=1)

    for b in range(srows // 8):
        for l in range(sub):
            low, high = src[l, 8 * b:8 * b + 8, :], src[sub + l, 8 * b:8 * b + 8, :]
            place = pl.ds(8 * b, 8)
            own[0][place, l, :] = jnp.where(lane_8 < width, low, swapped(high))
            own[1][place, l, :] = jnp.where(lane_8 < width, swapped(low), high)

    table_copy.wait()
    pl.semaphore_wait(barrier, total)

    def chain_copy(h, up, t):
        boxes = (ups if up else downs)[h]
        return pltpu.make_async_remote_copy(
            src_ref=own[h] if t == 0 else boxes[t - 1], dst_ref=boxes[t],
            send_sem=chain_send.at[h, 0 if up else 1, t], recv_sem=chain_recv.at[h, 0 if up else 1, t],
            device_id=(x, y + (inner if up else -inner), lev), device_id_type=MESH)

    def slot_copy(h, q, tile):
        c = lax.rem(column + q, columns)
        sem = (h * columns + q) * depth + tile
        return pltpu.make_async_remote_copy(
            src_ref=outbox.at[h, pl.ds((c * depth + tile) * capacity, capacity)],
            dst_ref=inboxes[h].at[pl.ds((column * depth + tile) * capacity, capacity)],
            send_sem=send_sem.at[sem], recv_sem=recv_sem.at[sem],
            device_id=column_id(c), device_id_type=MESH)

    def ship(h, chunk, tile):
        def fill(c, write):
            owner = c // inner * along_y + z * inner + lax.rem(c, inner)
            for j in range(capacity):
                write((c * depth + tile) * capacity + j, chunk[table[owner, tile * capacity + j]])

        def to_outbox(n, value):
            outbox[h, n] = value

        def to_inbox(n, value):
            inboxes[h][n] = value

        def peer(n, carry):
            q = jnp.where(lev % 2 == 0, n, columns - n)
            fill(lax.rem(column + q, columns), to_outbox)
            slot_copy(h, q, tile).start()
            return carry

        lax.fori_loop(1, columns, peer, 0)
        fill(column, to_inbox)

    def start_chain(h):
        if depth > 1:
            @pl.when(z < depth - 1)
            def _():
                chain_copy(h, True, 0).start()

            @pl.when(z > 0)
            def _():
                chain_copy(h, False, 0).start()

    def pass_on(h, t):
        for up, ok, onward in ((True, z >= t + 1, z < depth - 1), (False, z + 1 + t <= depth - 1, z > 0)):
            @pl.when(ok)
            def _():
                chain_copy(h, up, t).wait_recv()
                if t + 1 < depth - 1:
                    @pl.when(onward)
                    def _():
                        chain_copy(h, up, t + 1).start()
                ship(h, (ups if up else downs)[h][t], z - 1 - t if up else z + 1 + t)

    def s_copy(k):
        ok, device = near(*DIRS[k])
        return ok, pltpu.make_async_remote_copy(
            src_ref=smooth, dst_ref=s_in.at[OPPOSITE[k]], send_sem=s_send.at[k],
            recv_sem=s_recv.at[OPPOSITE[k]], device_id=device, device_id_type=MESH)

    def h_copy(k, tile):
        dx, dy = DIRS[k]
        ok, device = near(dx, dy)
        if dy == 0:
            source = main_a.at[pl.ds(frows if dx > 0 else PASSES, PASSES)]
            target = main_a.at[pl.ds(0 if dx > 0 else frows + PASSES, PASSES)]
        else:
            source, target = edge.at[tile], edge_in.at[OPPOSITE[k], tile]
        return ok, pltpu.make_async_remote_copy(
            src_ref=source, dst_ref=target, send_sem=h_send.at[k, tile],
            recv_sem=h_recv.at[OPPOSITE[k], tile], device_id=device, device_id_type=MESH)

    def split_weights(n):
        w_copy(n).wait()

        def one(i, carry):
            for k in range(fan):
                for h in range(HALVES):
                    value = w_full[i, pl.ds(k * LANES + h * width, width), :]
                    high = value.astype(jnp.bfloat16)
                    place = pl.ds(k * width, width)
                    w_high[h, i, place, :] = high
                    w_low[h, i, place, :] = (value - high.astype(jnp.float32)).astype(jnp.bfloat16)
            return carry

        lax.fori_loop(n * share, (n + 1) * share, one, 0)

    def product(h, i):
        rows = [[], []]
        for k in range(0, fan, 2):
            even, odd = (inboxes[h][pick[k + j, my_lane + i]] for j in range(2))
            rows[0].append(jnp.where(lane_8 < width, even, swapped(odd)))
            rows[1].append(jnp.where(lane_8 < width, swapped(even), odd))
        blocks = jnp.concatenate([jnp.concatenate(r, axis=1) for r in rows], axis=0)
        high = blocks.astype(jnp.bfloat16)
        low = (blocks - high.astype(jnp.float32)).astype(jnp.bfloat16)
        both = jnp.dot(jnp.concatenate([high, low], axis=0), w_high[h, i], preferred_element_type=jnp.float32)
        rest = jnp.dot(high, w_low[h, i], preferred_element_type=jnp.float32)
        result = both[:levels] + (both[levels:] + rest)
        if h == 0:
            main_a[PASSES + i] = result
        else:
            main_a[PASSES + i] += result

    groups = frows // GROUP

    def products(h, start, stop):
        def some(n, carry):
            for j in range(GROUP):
                product(h, n * GROUP + j)
            return carry

        lax.fori_loop(start, stop, some, 0)

    def landed(h):
        def one(n, carry):
            slot_copy(h, n // depth, lax.rem(n, depth)).wait_recv()
            return carry

        lax.fori_loop(depth, columns * depth, one, 0)

    start_chain(0)
    start_chain(1)
    ship(0, own[0], z)
    ship(1, own[1], z)
    for k in range(len(DIRS)):
        ok, copy = s_copy(k)

        @pl.when(ok)
        def _():
            copy.start()

    for k, (dx, dy) in enumerate(DIRS):
        ok, _ = near(dx, dy)

        @pl.when(jnp.logical_not(ok))
        def _():
            s_in[k] = jnp.zeros(s_in.shape[1:], jnp.float32)
            if dy == 0:
                main_a[pl.ds(0 if dx < 0 else frows + PASSES, PASSES)] = jnp.zeros(
                    (PASSES,) + main_a.shape[1:], jnp.float32)
            else:
                edge_in[k] = jnp.zeros(edge_in.shape[1:], jnp.float32)

    span = pl.ds(pl.multiple_of(me // groups_in_tile * LANES, LANES), LANES)
    every = lax.broadcasted_iota(jnp.int32, (along_x * along_y, LANES), 0)
    named = [devices[k:k + 1, span] for k in range(fan)]
    hits = [jnp.where(named[k] == every, 1.0, 0.0) for k in range(fan)]
    found = ranks(hits)
    for k in range(fan):
        rank = jnp.sum(hits[k] * found[k], axis=0, keepdims=True).astype(jnp.int32)
        tile_y = lax.rem(named[k], along_y)
        base = (named[k] // along_y * inner + lax.rem(tile_y, inner)) * depth + tile_y // inner
        pick_v[k:k + 1, :] = jnp.clip(base * capacity + rank, 0, columns * depth * capacity - 1)
    pick_copy.start()

    done = 0
    events = sorted((t + 0.5 * h, h, t) for h in range(HALVES) for t in range(depth - 1))
    for _, h, t in events:
        pass_on(h, t)
        if done < W_PIECES:
            split_weights(done)
            done += 1
    for n in range(done, W_PIECES):
        split_weights(n)

    for k in range(len(DIRS)):
        ok, copy = s_copy(k)

        @pl.when(ok)
        def _():
            copy.wait_send()
            arrival_wait(s_in.at[k], smooth, s_recv.at[k])

    row_lane = lax.broadcasted_iota(jnp.int32, (1, LANES), 1)

    def side(left, right):
        return jnp.where(row_lane < PASSES, right, jnp.where(row_lane >= LANES - PASSES, left, 0.0))

    for i in range(frows):
        s_main[PASSES + i] = smooth[i:i + 1, :]
        s_side[PASSES + i] = side(s_in[at[0, -1], i:i + 1, :], s_in[at[0, 1], i:i + 1, :])
    for i in range(PASSES):
        low, high = frows - PASSES + i, frows + PASSES + i
        s_main[i] = s_in[at[-1, 0], low:low + 1, :]
        s_side[i] = side(s_in[at[-1, -1], low:low + 1, :], s_in[at[-1, 1], low:low + 1, :])
        s_main[high] = s_in[at[1, 0], i:i + 1, :]
        s_side[high] = side(s_in[at[1, -1], i:i + 1, :], s_in[at[1, 1], i:i + 1, :])

    landed(0)
    pick_copy.wait()
    products(0, 0, groups)
    landed(1)

    def send_halo(wanted):
        for k, (dx, dy) in enumerate(DIRS):
            for tile in wanted(dx, dy):
                ok, copy = h_copy(k, tile)

                @pl.when(ok)
                def _():
                    copy.start()

    def halo_tiles(dx, dy):
        if dy == 0:
            return [0]
        return list(range(tiles)) if dx == 0 else [0 if dx < 0 else tiles - 1]

    def pack(b):
        packed = jnp.zeros((levels, LANES), jnp.float32)
        for j in range(PER_TILE):
            moved = pltpu.roll(main_a[PASSES + b * PER_TILE + j], STRIP * j + STRIP // 2, axis=1)
            packed = jnp.where(lane // STRIP == j, moved, packed)
        edge[b] = packed
        send_halo(lambda dx, dy: [b] if dy != 0 and b in halo_tiles(dx, dy) else [])

    products(1, 0, 1)
    products(1, groups - 1, groups)
    send_halo(lambda dx, dy: [0] if dy == 0 else [])
    for b in range(tiles):
        products(1, max(1, b * groups // tiles), min(groups - 1, (b + 1) * groups // tiles))
        pack(b)

    def sent(n, carry):
        for h in range(HALVES):
            slot_copy(h, n // depth, lax.rem(n, depth)).wait_send()
        return carry

    lax.fori_loop(depth, columns * depth, sent, 0)
    for t in range(depth - 1):
        for h in range(HALVES):
            @pl.when(jnp.logical_and(z < depth - 1, z - t >= 0))
            def _():
                chain_copy(h, True, t).wait_send()

            @pl.when(jnp.logical_and(z > 0, z + t <= depth - 1))
            def _():
                chain_copy(h, False, t).wait_send()

    for k, (dx, dy) in enumerate(DIRS):
        for tile in halo_tiles(dx, dy):
            ok, copy = h_copy(k, tile)

            @pl.when(ok)
            def _():
                copy.wait_send()

        for tile in halo_tiles(-dx, -dy):
            @pl.when(near(dx, dy)[0])
            def _():
                if dy == 0:
                    rows = main_a.at[pl.ds(0 if dx < 0 else frows + PASSES, PASSES)]
                    arrival_wait(rows, rows, h_recv.at[k, tile])
                else:
                    arrival_wait(edge_in.at[k, tile], edge.at[tile], h_recv.at[k, tile])

    inside = jnp.logical_or(lane < PASSES, lane >= LANES - PASSES)

    def unpack(row, tile, place, left, right):
        merged = jnp.where(lax.rem(lane, STRIP) < STRIP // 2, edge_in[left, tile], edge_in[right, tile])
        moved = pltpu.roll(merged, (2 * LANES - STRIP * place - STRIP // 2) % LANES, axis=1)
        side_a[row] = jnp.where(inside, moved, 0.0)

    for i in range(frows):
        unpack(PASSES + i, i // PER_TILE, i % PER_TILE, at[0, -1], at[0, 1])
    for i in range(PASSES):
        far = frows - PASSES + i
        unpack(i, far // PER_TILE, far % PER_TILE, at[-1, -1], at[-1, 1])
        unpack(frows + PASSES + i, 0, i, at[1, -1], at[1, 1])

    first, last = lane == 0, lane == LANES - 1

    def smooth_row(r, main, sides, write):
        u, h = main[r], sides[r]
        u_up, u_down = pltpu.roll(u, 1, axis=1), pltpu.roll(u, LANES - 1, axis=1)
        h_up, h_down = pltpu.roll(h, 1, axis=1), pltpu.roll(h, LANES - 1, axis=1)
        lap = (main[r + 1] + main[r - 1] + jnp.where(last, h_down, u_down)
               + jnp.where(first, h_up, u_up) - 4.0 * u)
        lap_h = (sides[r + 1] + sides[r - 1] + jnp.where(last, u_down, h_down)
                 + jnp.where(first, u_up, h_up) - 4.0 * h)
        write(r, u, s_main[r] * lap, h + s_side[r] * lap_h)

    def write_b(r, u, step, h):
        main_b[r] = u + step
        side_b[r] = h

    def write_a(r, u, step, h):
        main_a[r] = u + step
        side_a[r] = h

    def write_out(r, u, step, h):
        out[pl.ds(r - PASSES, levels, stride=frows), :] = u + step

    for p, (main, sides, write) in enumerate((
            (main_a, side_a, write_b), (main_b, side_b, write_a), (main_a, side_a, write_out))):
        start, count = p + 1, frows + 2 * PASSES - 2 * (p + 1)
        chunk = next(n for n in (12, 17, 16, 2, 1) if count % n == 0)

        def rows(n, carry):
            for j in range(chunk):
                smooth_row(start + n * chunk + j, main, sides, write)
            return carry

        lax.fori_loop(0, count // chunk, rows, 0)


def arrival_wait(target, source, sem):
    pltpu.make_async_copy(source, target, sem).wait()


def shards(source, remap_weights, intersection_devices, intersection_rows, smoothing):
    along_x = lax.axis_size("gx")
    along_y = lax.axis_size("gy")
    devices = along_x * along_y
    frows, fanin, block = remap_weights.shape[:3]
    levels, srows = source.shape[:2]
    capacity = 2 * max(1, frows * fanin // devices)
    depth, inner = layout(along_x, along_y, capacity, srows)
    columns = along_x * inner
    full = frows + 2 * PASSES
    sub = levels // HALVES
    vmem = functools.partial(pltpu.VMEM, dtype=jnp.float32)
    tile = (levels, block)
    in_vmem = pl.BlockSpec(memory_space=pltpu.VMEM)
    anywhere = pl.BlockSpec(memory_space=pl.ANY)
    entries = (fanin, intersection_devices.shape[0])
    tables = ((devices, -(-depth * capacity // block) * block), (fanin, block))
    slots_all = columns * depth * capacity
    dma = pltpu.SemaphoreType.DMA
    sides = len(DIRS)
    edges = frows // PER_TILE
    halves = pltpu.VMEM((HALVES, frows, fanin * block // HALVES, block), jnp.bfloat16)
    field = pl.pallas_call(
        functools.partial(kernel, (along_x, along_y, depth, inner, capacity)),
        out_shape=jax.ShapeDtypeStruct((levels * frows, block), jnp.float32),
        in_specs=[anywhere] * 5,
        out_specs=in_vmem,
        scratch_shapes=[
            pltpu.VMEM(entries, jnp.int32), pltpu.VMEM(entries, jnp.int32),
            vmem((levels, srows, block)), vmem((frows, block)),
            *[pltpu.VMEM(shape, jnp.int32) for shape in tables],
            *[pltpu.SMEM(shape, jnp.int32) for shape in tables],
            vmem((slots_all, sub, block)), vmem((slots_all, sub, block)),
            vmem((HALVES, slots_all, sub, block)),
            vmem((frows, fanin * block, block)),
            halves, halves,
            vmem((full,) + tile), vmem((full,) + tile), vmem((full,) + tile), vmem((full,) + tile),
            vmem((full, 1, block)), vmem((full, 1, block)),
            vmem((sides, frows, block)),
            vmem((edges,) + tile),
            vmem((sides, edges) + tile),
            dma((HALVES * columns * depth,)), dma((HALVES * columns * depth,)),
            dma((HALVES, 2, max(1, depth - 1))), dma((HALVES, 2, max(1, depth - 1))),
            dma((sides,)), dma((sides,)), dma((sides, edges)), dma((sides, edges)),
            dma((W_PIECES,)), dma((6,)),
        ] + [vmem((srows, sub, block))] * (HALVES + 2 * HALVES * (depth - 1)),
        compiler_params=pltpu.CompilerParams(
            collective_id=0, has_side_effects=True, vmem_limit_bytes=56 * 2 ** 20),
        cost_estimate=pl.CostEstimate(
            flops=6 * levels * frows * fanin * block * block, bytes_accessed=16 * 2 ** 20, transcendentals=0),
    )(intersection_devices.T, intersection_rows.T, source, remap_weights.reshape(frows, fanin * block, block), smoothing)
    return field.reshape(levels, frows, block)


def solution(mesh):
    return jax.shard_map(
        shards,
        mesh=mesh,
        in_specs=(P("lev", "gy", "gx"), P(("gx", "gy"), None, None, None), P(), P(), P("gx", "gy")),
        out_specs=P("lev", "gx", "gy"),
        check_vma=False,
    )
```
